256 devices in a mesh: gx: 8 (over x, core), gy: 4 (over y), gz: 8 (over z).
Axes of the slice: x: 4, y: 4, z: 8, core: 2. Of those that a mesh axis runs over, the one named last changes fastest.
Arguments:
- conserved: float32 [1024, 5, 4096], P(('gx', 'gy', 'gz')), as said below
- old_owner: int32 [512], replicated, may hold values from 0 to 255, as said below
- new_owner: int32 [512], replicated, may hold values from 0 to 255, as said below
- box_level: int32 [512], replicated, may hold values from 0 to 2
- face_source: int32 [1024, 6], P(('gx', 'gy', 'gz')), may hold values from 0 to 7, as said below
- coarse_part: int32 [1024, 6], P(('gx', 'gy', 'gz')), may hold values from 0 to 4
Outputs:
- new_state: float32 [768, 5, 4096], P(('gx', 'gy', 'gz'))
The draws below stay inside these ranges and needn't reach their ends.
Inputs may be any that keep to these rules, and one draw needn't show every extreme that they name: Boxes are numbered along a Morton curve and old_owner never falls along the numbering. Every device owns 1 to 4 boxes before regridding, and some device owns exactly 4. `new_owner`: each box's new owner is its old owner or one of the two devices next to it in the device order. The boxes that a device passes to its lower neighbour are the first ones it owned, those it passes to its upper neighbour the last ones. At most 1 box crosses each boundary between consecutive devices in each direction; all boundaries but three carry exactly 1 in each direction. Every device owns 1 to 3 boxes after regridding, and some device owns exactly 3. For every occupied old slot, the slot that face_source names is occupied. Entries of empty slots also lie in the range. `conserved`: in every cell of every slot the density and the pressure 0.4 (energy - |momentum|^2 / (2 density)) lie between 0.3 and 3, and each velocity component between -1.5 and 1.5.
All inputs are finite; a program needn't handle non-finite values.
Results may differ from the reference program's by a relative error of at most 0.0003.
Values sent between devices are 32-bit elements; how exact they have to be, the bound alone decides.
No kernel may reach another device: no remote copies, remote signals or barrier semaphores. Data moves between devices by JAX's collectives and lax.ppermute only.
A program may use at most 128 MiB of HBM per device.

```python
import math
import jax
import jax.numpy as jnp
from jax import lax

EDGE = 16
DEPTH = 4
FIELDS = 5
BOX_DEV = 2
OLD_CAP = 4
NEW_CAP = 3
NBOX = 512
SLOTS = 1024
N_GX = 8
N_GY = 4
N_GZ = 8


GAMMA = 1.4


def layout(key):
    devices = N_GX * N_GY * N_GZ
    move_cap = BOX_DEV // 2
    chosen = jax.random.randint(key, (), 3, devices // 2 - 4)
    fuller = chosen + devices // 2
    emptier = fuller + 2
    boundaries = jnp.arange(devices + 1, dtype=jnp.int32)
    inner = (boundaries >= 1) & (boundaries <= devices - 1)
    upward = jnp.where(inner, move_cap, 0)
    upward = jnp.where((boundaries == chosen) | (boundaries == emptier), 0, upward)
    downward = jnp.where(inner, move_cap, 0)
    downward = jnp.where(boundaries == chosen + 1, 0, downward)
    device_ids = jnp.arange(devices, dtype=jnp.int32)
    new_counts = BOX_DEV + jnp.where(device_ids == fuller, 1, 0) - jnp.where(device_ids == emptier, 1, 0)
    old_counts = new_counts + upward[1:] + downward[:-1] - upward[:-1] - downward[1:]
    old_start = jnp.concatenate([jnp.zeros((1,), jnp.int32), jnp.cumsum(old_counts).astype(jnp.int32)])
    box_ids = jnp.arange(NBOX, dtype=jnp.int32)
    old_owner = jnp.sum((old_start[1:devices][None, :] <= box_ids[:, None]).astype(jnp.int32), axis=1)
    rank = box_ids - old_start[old_owner]
    goes_down = rank < downward[old_owner]
    goes_up = rank >= old_counts[old_owner] - upward[old_owner + 1]
    new_owner = jnp.where(goes_down, old_owner - 1, jnp.where(goes_up, old_owner + 1, old_owner))
    return (old_start, old_owner, new_owner.astype(jnp.int32), chosen)


def draw_old_owner(key, part):
    old_start, old_owner, new_owner, chosen = layout(key)
    key = jax.random.fold_in(key, 11)
    return old_owner


def draw_new_owner(key, part):
    old_start, old_owner, new_owner, chosen = layout(key)
    key = jax.random.fold_in(key, 14)
    return new_owner


def draw_face_source(key, part):
    old_start, old_owner, new_owner, chosen = layout(key)
    key = jax.random.fold_in(key, 12)
    counts = old_start[1:] - old_start[:-1]
    key_home, key_slot = jax.random.split(key)
    slot_rows = jnp.arange(SLOTS, dtype=jnp.int32)
    home_device = slot_rows // OLD_CAP
    axis_sizes = (N_GX, N_GY, N_GZ)
    axis_strides = (N_GY * N_GZ, N_GZ, 1)
    on_home = jax.random.randint(key_home, (SLOTS, 6), 0, 2)
    raw_slot = jax.random.randint(key_slot, (SLOTS, 6), 0, 1 << 20)
    columns = []
    for face_index in range(6):
        normal = face_index // 2
        offset_step = -1 if face_index % 2 == 0 else 1
        coordinate = home_device // axis_strides[normal] % axis_sizes[normal]
        beside = home_device + ((coordinate + offset_step) % axis_sizes[normal] - coordinate) * axis_strides[normal]
        home_pick = OLD_CAP + raw_slot[:, face_index] % counts[home_device]
        beside_pick = raw_slot[:, face_index] % counts[beside]
        columns.append(jnp.where(on_home[:, face_index] == 1, home_pick, beside_pick))
    table = jnp.stack(columns, axis=1)
    forced = (slot_rows[:, None] == chosen * OLD_CAP) & (jnp.arange(6)[None, :] == 0)
    return jnp.where(forced, 2 * OLD_CAP - 1, table)


def draw_coarse_part(key, part):
    key = jax.random.fold_in(key, 13)
    raw_code = jax.random.randint(key, (SLOTS, 6), 0, 16)
    return jnp.where(raw_code >= 12, raw_code - 11, 0)


def draw_conserved(key, part):
    key = jax.random.fold_in(key, 15)
    key_density, key_velocity, key_pressure = jax.random.split(key, 3)
    box_count = N_GX * N_GY * N_GZ * OLD_CAP
    volume = EDGE ** 3
    low_log = math.log(0.3)
    high_log = math.log(3.0)
    density = jnp.exp(jax.random.uniform(key_density, (box_count, volume), jnp.float32, low_log, high_log))
    velocity = jnp.clip(0.5 * jax.random.normal(key_velocity, (box_count, 3, volume), jnp.float32), -1.5, 1.5)
    pressure = jnp.exp(jax.random.uniform(key_pressure, (box_count, volume), jnp.float32, low_log, high_log))
    momentum = density[:, None] * velocity
    energy = pressure / (GAMMA - 1.0) + 0.5 * density * jnp.sum(velocity * velocity, axis=1)
    return jnp.concatenate([density[:, None], momentum, energy[:, None]], axis=1)


def set_ends(values, own_key, smallest, largest):
    shape = values.shape
    place = [jax.random.randint(jax.random.fold_in(own_key, axis), (), 0, shape[axis]) for axis in range(len(shape))]
    values = values.at[tuple(place)].set(smallest)
    longest = shape.index(max(shape))
    place[longest] = (place[longest] + 1) % shape[longest]
    return values.at[tuple(place)].set(largest)


def setup_inputs(seed: int = 0) -> dict:
    seeds = jax.random.split(jax.random.key(seed), 7)
    return {
        "conserved": draw_conserved(jax.random.fold_in(seeds[6], 71), 0),
        "old_owner": draw_old_owner(jax.random.fold_in(seeds[6], 71), 0),
        "new_owner": draw_new_owner(jax.random.fold_in(seeds[6], 71), 0),
        "box_level": set_ends(jax.random.randint(seeds[3], (NBOX,), 0, 3), jax.random.fold_in(seeds[3], 1), 0, 2).astype(jnp.int32),
        "face_source": draw_face_source(jax.random.fold_in(seeds[6], 71), 0),
        "coarse_part": draw_coarse_part(jax.random.fold_in(seeds[6], 71), 0),
    }


GAMMA = 1.4
STEP_RATIO = 0.02
FLATTEN_WEIGHT = 2.0

def level_scale(levels):
    return STEP_RATIO * jnp.where(levels == 0, 1.0, jnp.where(levels == 1, 2.0, 4.0)).astype(jnp.float32)

def axis_first(box_cells, normal):
    count_boxes, fields, edge_cells = (box_cells.shape[0], box_cells.shape[1], box_cells.shape[2])
    if normal == 0:
        turned = box_cells
    elif normal == 1:
        turned = jnp.transpose(box_cells, (0, 1, 3, 2, 4))
    else:
        turned = jnp.transpose(box_cells, (0, 1, 4, 2, 3))
    return turned.reshape(count_boxes, fields, edge_cells, edge_cells * edge_cells)

def axis_back(line_cells, normal):
    count_boxes, fields, edge_cells = (line_cells.shape[0], line_cells.shape[1], line_cells.shape[2])
    box_cells = line_cells.reshape(count_boxes, fields, edge_cells, edge_cells, edge_cells)
    if normal == 1:
        box_cells = jnp.transpose(box_cells, (0, 1, 3, 2, 4))
    elif normal == 2:
        box_cells = jnp.transpose(box_cells, (0, 1, 3, 4, 2))
    return box_cells.reshape(count_boxes, fields, edge_cells ** 3)

def make_ghost(face_layer, coarse_code, which_side, edge_cells):
    count_boxes, fields, depth_cells, area_cells = face_layer.shape
    half_edge = edge_cells // 2
    if which_side == 0:
        depth_rows = (2, 2, 3, 3)
    else:
        depth_rows = (0, 0, 1, 1)
    coarse = jnp.stack([face_layer[:, :, row_index] for row_index in depth_rows], axis=2)
    blocks = coarse.reshape(count_boxes, fields, depth_cells, 2, half_edge, 2, half_edge)
    quadrant = coarse_code - 1
    upper_first = (quadrant // 2 == 1)[:, None, None, None, None, None]
    halves = jnp.where(upper_first, blocks[:, :, :, 1], blocks[:, :, :, 0])
    upper_second = (quadrant % 2 == 1)[:, None, None, None, None]
    quarter = jnp.where(upper_second, halves[:, :, :, :, 1], halves[:, :, :, :, 0])
    widened = jnp.repeat(jnp.repeat(quarter, 2, axis=3), 2, axis=4)
    widened = widened.reshape(count_boxes, fields, depth_cells, area_cells)
    return jnp.where((coarse_code > 0)[:, None, None, None], widened, face_layer)

def flux_and_state(primitive, normal):
    density = primitive[:, 0]
    velocity = primitive[:, 1:4]
    pressure = primitive[:, 4]
    normal_speed = primitive[:, 1 + normal]
    energy = pressure / (GAMMA - 1.0) + 0.5 * density * lax.optimization_barrier(jnp.sum(velocity * velocity, axis=1))
    state_vec = jnp.concatenate([density[:, None], density[:, None] * velocity, energy[:, None]], axis=1)
    zero_part = jnp.zeros_like(pressure)
    pushes = [zero_part, zero_part, zero_part, zero_part, normal_speed * pressure]
    pushes[1 + normal] = pressure
    face_flux = normal_speed[:, None] * state_vec + jnp.stack(pushes, axis=1)
    return (state_vec, face_flux)

def star_flux(primitive, state_vec, face_flux, wave, mid_wave, denom, normal):
    density = primitive[:, 0]
    normal_speed = primitive[:, 1 + normal]
    pressure = primitive[:, 4]
    mass_rate = density * (wave - normal_speed)
    pieces = [jnp.ones_like(density), primitive[:, 1], primitive[:, 2], primitive[:, 3]]
    pieces[1 + normal] = mid_wave
    pieces.append(state_vec[:, 4] / density + (mid_wave - normal_speed) * (mid_wave + pressure / mass_rate))
    star_vec = jnp.stack(pieces, axis=1) * mass_rate[:, None]
    return face_flux + (wave / denom)[:, None] * star_vec - wave[:, None] * state_vec

def riemann_flux(left_prim, right_prim, normal):
    left_density, left_speed, left_pressure = (left_prim[:, 0], left_prim[:, 1 + normal], left_prim[:, 4])
    right_density, right_speed, right_pressure = (right_prim[:, 0], right_prim[:, 1 + normal], right_prim[:, 4])
    left_sound = jnp.sqrt(GAMMA * left_pressure / left_density)
    right_sound = jnp.sqrt(GAMMA * right_pressure / right_density)
    slow_wave = jnp.minimum(left_speed - left_sound, right_speed - right_sound)
    fast_wave = jnp.maximum(left_speed + left_sound, right_speed + right_sound)
    left_mass = left_density * (slow_wave - left_speed)
    right_mass = right_density * (fast_wave - right_speed)
    mid_wave = (right_pressure - left_pressure + left_mass * left_speed - right_mass * right_speed) / (left_mass - right_mass)
    left_state, left_flux = flux_and_state(left_prim, normal)
    right_state, right_flux = flux_and_state(right_prim, normal)
    left_used = (slow_wave < 0.0) & (mid_wave >= 0.0)
    right_used = (mid_wave < 0.0) & (fast_wave > 0.0)
    left_denom = jnp.where(left_used, slow_wave - mid_wave, -1.0)
    right_denom = jnp.where(right_used, fast_wave - mid_wave, 1.0)
    left_star = star_flux(left_prim, left_state, left_flux, slow_wave, mid_wave, left_denom, normal)
    right_star = star_flux(right_prim, right_state, right_flux, fast_wave, mid_wave, right_denom, normal)
    return jnp.where((slow_wave >= 0.0)[:, None], left_flux, jnp.where((mid_wave >= 0.0)[:, None], left_star, jnp.where((fast_wave > 0.0)[:, None], right_star, right_flux)))

def sweep_axis(line_cells, normal):
    length = line_cells.shape[2]
    density = line_cells[:, 0]
    velocity = line_cells[:, 1:4] / density[:, None]
    pressure = (GAMMA - 1.0) * (line_cells[:, 4] - 0.5 * density * lax.optimization_barrier(jnp.sum(velocity * velocity, axis=1)))
    primitive = jnp.concatenate([density[:, None], velocity, pressure[:, None]], axis=1)
    pressure_jump = jnp.abs(pressure[:, 3:length - 1] - pressure[:, 1:length - 3])
    pressure_sum = pressure[:, 4:] + pressure[:, :length - 4]
    flatten = jnp.clip(1.0 - FLATTEN_WEIGHT * pressure_jump / pressure_sum, 0.0, 1.0)
    flatten_min = jnp.minimum(jnp.minimum(flatten[:, :length - 6], flatten[:, 1:length - 5]), flatten[:, 2:])
    centre = primitive[:, :, 3:length - 3]
    back_diff = centre - primitive[:, :, 2:length - 4]
    ahead_diff = primitive[:, :, 4:length - 2] - centre
    limited = jnp.minimum(jnp.minimum(0.5 * jnp.abs(back_diff + ahead_diff), 2.0 * jnp.abs(back_diff)), 2.0 * jnp.abs(ahead_diff))
    slopes = jnp.where(back_diff * ahead_diff > 0.0, jnp.sign(back_diff) * limited, 0.0) * flatten_min[:, None]
    left_prim = centre[:, :, :-1] + 0.5 * slopes[:, :, :-1]
    right_prim = centre[:, :, 1:] - 0.5 * slopes[:, :, 1:]
    face_flux = riemann_flux(left_prim, right_prim, normal)
    return face_flux[:, :, 1:] - face_flux[:, :, :-1]

def advance(interior, ghosts, step_scale, edge_cells):
    count_boxes, fields = (interior.shape[0], interior.shape[1])
    box_cells = interior.reshape(count_boxes, fields, edge_cells, edge_cells, edge_cells)
    change = jnp.zeros_like(interior)
    for normal in range(3):
        lower_ghost = ghosts[:, :, 2 * normal].reshape(count_boxes, fields, DEPTH, edge_cells * edge_cells)
        upper_ghost = ghosts[:, :, 2 * normal + 1].reshape(count_boxes, fields, DEPTH, edge_cells * edge_cells)
        line_cells = jnp.concatenate([lower_ghost, axis_first(box_cells, normal), upper_ghost], axis=2)
        change = change + axis_back(sweep_axis(line_cells, normal), normal)
    return interior - step_scale[:, None, None] * change

def reference(conserved, old_owner, new_owner, box_level, face_source, coarse_part):
    devices = N_GX * N_GY * N_GZ
    edge_cells = EDGE
    boundaries = jnp.arange(devices + 1, dtype=jnp.int32)
    old_start = lax.optimization_barrier(jnp.sum((old_owner[None, :] < boundaries[:, None]).astype(jnp.int32), axis=1))
    all_ids = jnp.arange(NBOX, dtype=jnp.int32)
    axis_sizes = (N_GX, N_GY, N_GZ)
    axis_strides = (N_GY * N_GZ, N_GZ, 1)

    def one_device(device):
        new_slots = jnp.arange(NEW_CAP, dtype=jnp.int32)
        mine = new_owner == device
        ranks = jnp.cumsum(mine.astype(jnp.int32)) - 1
        count_mine = jnp.sum(mine.astype(jnp.int32))
        match = mine[None, :] & (ranks[None, :] == new_slots[:, None])
        box_ids = lax.optimization_barrier(jnp.sum(jnp.where(match, all_ids[None, :], 0), axis=1)).astype(jnp.int32)
        filled = new_slots < count_mine
        home_device = old_owner[box_ids]
        box_rows = home_device * OLD_CAP + box_ids - old_start[home_device]
        interior = conserved[box_rows]
        ghost_list = []
        for face_index in range(6):
            normal = face_index // 2
            which_side = face_index % 2
            source = face_source[box_rows, face_index]
            coordinate = home_device // axis_strides[normal] % axis_sizes[normal]
            offset_step = -1 if which_side == 0 else 1
            beside = home_device + ((coordinate + offset_step) % axis_sizes[normal] - coordinate) * axis_strides[normal]
            on_home = source >= OLD_CAP
            source_rows = jnp.where(on_home, home_device * OLD_CAP + source - OLD_CAP, beside * OLD_CAP + source)
            source_box = conserved[source_rows].reshape(NEW_CAP, FIELDS, edge_cells, edge_cells, edge_cells)
            turned = axis_first(source_box, normal)
            if which_side == 0:
                face_layer = turned[:, :, edge_cells - DEPTH:]
            else:
                face_layer = turned[:, :, :DEPTH]
            ghost_list.append(make_ghost(face_layer, coarse_part[box_rows, face_index], which_side, edge_cells))
        ghosts = jnp.stack(ghost_list, axis=2).reshape(NEW_CAP, FIELDS, 6, DEPTH * edge_cells * edge_cells)
        updated = advance(interior, ghosts, level_scale(box_level[box_ids]), edge_cells)
        return jnp.where(filled[:, None, None], updated, 0.0)
    result = lax.map(one_device, jnp.arange(devices, dtype=jnp.int32))
    return result.reshape(devices * NEW_CAP, FIELDS, edge_cells ** 3)
```

```python
import functools

import jax
import jax.numpy as jnp
from jax import lax
from jax.experimental import pallas as pl
from jax.experimental.pallas import tpu as pltpu
from jax.sharding import PartitionSpec as P

EDGE = 16
FIELDS = 5
LANES = 128
SUB = 8
PLANE = EDGE * SUB
FACE_ROWS = FIELDS * 4 * SUB
AXES = ("gx", "gy", "gz")
ORDER = ((0, 1, 2, 3, 4), (0, 2, 1, 3, 4), (0, 3, 1, 2, 4))
FACES = 17
FACE_CHUNK = 3
VMEM_LIMIT = 48 * 1024 * 1024


def iota(axis):
    return lax.broadcasted_iota(jnp.int32, (SUB, LANES), axis)


def swap_bit(rows, bit, axis, step):
    size = (SUB, LANES)[axis]
    low = (iota(axis) & step) == 0
    out = list(rows)
    for i in range(len(rows)):
        if i & bit:
            continue
        j = i | bit
        a, b = rows[i], rows[j]
        out[i] = jnp.where(low, a, pltpu.roll(b, step, axis))
        out[j] = jnp.where(low, pltpu.roll(a, size - step, axis), b)
    return out


def swap_xy(rows):
    rows = swap_bit(rows, 8, 0, 1)
    for bit, step in ((4, 64), (2, 32), (1, 16)):
        rows = swap_bit(rows, bit, 1, step)
    return rows


def swap_xz(rows):
    for bit, step in ((8, 8), (4, 4), (2, 2), (1, 1)):
        rows = swap_bit(rows, bit, 1, step)
    return rows


def primitives(rho, mx, my, mz, energy):
    inv = 1.0 / rho
    u, v, w = mx * inv, my * inv, mz * inv
    p = 0.4 * (energy - 0.5 * rho * (u * u + v * v + w * w))
    return rho, u, v, w, p


def tile(ref, row):
    return ref[pl.ds(pl.multiple_of(row, SUB), SUB), :]


def layers_kernel(cons_ref, c_ref, sx0, sx1, sy0, sy1, sz0, sz1, w_ref):
    for b in range(4):
        for k in range(2 * EDGE):
            x, t = k // 2, k % 2
            c_ref[pl.ds(x * SUB + 2 * b + t, FIELDS, stride=PLANE), :] = cons_ref[
                b, :, k * LANES : (k + 1) * LANES
            ]
    for x in range(EDGE):
        got = [c_ref[f * PLANE + x * SUB : f * PLANE + (x + 1) * SUB, :] for f in range(FIELDS)]
        for f, value in enumerate(primitives(*got)):
            w_ref[f * PLANE + x * SUB : f * PLANE + (x + 1) * SUB, :] = value

    def field(f, carry):
        rows = [tile(w_ref, f * PLANE + x * SUB) for x in range(EDGE)]
        turned = (rows, swap_xy(rows), swap_xz(rows))
        for got, low, high in zip(turned, (sx0, sy0, sz0), (sx1, sy1, sz1)):
            for r in range(4):
                place = pl.ds(pl.multiple_of(f * 4 * SUB + r * SUB, SUB), SUB)
                low[place, :] = got[r]
                high[place, :] = got[EDGE - 4 + r]
        return carry

    lax.fori_loop(0, FIELDS, field, 0)


def device_position():
    place = lax.axis_index(AXES[0])
    for axis in AXES[1:]:
        place = place * lax.axis_size(axis) + lax.axis_index(axis)
    return place


def find_boxes(old_ref, new_ref):
    boxes = old_ref.shape[0]
    place = device_position()

    def halve(_, ends):
        low, high = ends
        middle = (low + high) // 2
        below = old_ref[jnp.minimum(middle, boxes - 1)] < place
        open_ends = low < high
        return (
            jnp.where(open_ends & below, middle + 1, low),
            jnp.where(open_ends & jnp.logical_not(below), middle, high),
        )

    steps = boxes.bit_length()
    low, _ = lax.fori_loop(0, steps, halve, (jnp.int32(0), jnp.int32(boxes)))
    count = jnp.int32(0)
    for k in range(4):
        at = low + k
        mine = (at < boxes) & (old_ref[jnp.minimum(at, boxes - 1)] == place)
        count = count + mine.astype(jnp.int32)
    high = low + count
    before = jnp.maximum(low - 1, 0)
    after = jnp.minimum(high, boxes - 1)
    up_in = ((low > 0) & (new_ref[before] == place)).astype(jnp.int32)
    down_in = ((high < boxes) & (new_ref[after] == place)).astype(jnp.int32)
    down_out = (new_ref[low] == place - 1).astype(jnp.int32)
    up_out = (new_ref[high - 1] == place + 1).astype(jnp.int32)
    return low, high, up_in, down_in, down_out, up_out


def ghosts_kernel(
    old_ref, new_ref, level_ref, source_ref, coarse_ref, c_ref, *refs
):
    own = refs[0:6]
    got = refs[6:12]
    info_ref, g_ref, up_ref, down_ref = refs[12:16]
    low, high, up_in, down_in, down_out, up_out = find_boxes(old_ref, new_ref)
    boxes = old_ref.shape[0]
    count = high - low
    staying = count - down_out - up_out
    info_ref[0] = up_in
    info_ref[1] = up_in + staying
    info_ref[2] = up_in + staying + down_in
    info_ref[3] = down_out - up_in
    for j in range(3):
        box = jnp.where(
            j < up_in,
            low - 1,
            jnp.where(j < up_in + staying, low + down_out + j - up_in, high + j - up_in - staying),
        )
        info_ref[4 + j] = level_ref[jnp.clip(box, 0, boxes - 1)]

    sub, lane = iota(0), iota(1)
    half = sub & 1
    for face in range(6):
        axis, side = face // 2, face % 2
        slot_rows = jnp.zeros((SUB, LANES), jnp.int32)
        codes = jnp.zeros((SUB, LANES), jnp.int32)
        for b in range(4):
            here = (sub >> 1) == b
            slot_rows = jnp.where(here, source_ref[b, face], slot_rows)
            codes = jnp.where(here, coarse_ref[b, face], codes)
        is_own = slot_rows >= 4
        is_coarse = codes > 0
        quadrant = codes - 1
        first, second = (quadrant >> 1) & 1, quadrant & 1
        if axis == 2:
            first, second = second, first
        from_row = 2 * (slot_rows & 3) + jnp.where(is_coarse, first, half)
        from_lane = jnp.where(
            is_coarse,
            (half * 4 + (lane >> 5)) * EDGE + second * 8 + ((lane & 15) >> 1),
            lane,
        )
        mine = own[2 * axis + 1 - side]
        theirs = got[face]
        for f in range(FIELDS):
            picked = []
            for r in range(4):
                place = slice((f * 4 + r) * SUB, (f * 4 + r + 1) * SUB)
                picked.append(
                    jnp.where(
                        is_own,
                        jnp.take_along_axis(mine[place, :], from_row, axis=0),
                        jnp.take_along_axis(theirs[place, :], from_row, axis=0),
                    )
                )
            for k in range(4):
                source = picked[(2 if side == 0 else 0) + k // 2]
                chosen = jnp.where(is_coarse, source, picked[k])
                row = face * FACE_ROWS + (f * 4 + k) * SUB
                g_ref[row : row + SUB, :] = jnp.take_along_axis(chosen, from_lane, axis=1)

    for slot, out in ((count - 1, up_ref), (jnp.int32(0), down_ref)):
        for t in range(2):
            for n in range(25):
                source, group = (c_ref, n) if n < 10 else (g_ref, n - 10)
                out[(t * 25 + n) * SUB : (t * 25 + n + 1) * SUB, :] = source[
                    pl.ds(group * 64 + 2 * slot + t, SUB, stride=SUB), :
                ]


def advance_kernel(
    info_ref,
    c_ref,
    g_ref,
    lower_ref,
    upper_ref,
    out_ref,
    cn_ref,
    gn_ref,
    line_ref,
    left_ref,
    right_ref,
    flux_ref,
):
    def fill(j, carry):
        start = 2 * j

        def put(n, t, value):
            target, group = (cn_ref, n) if n < 10 else (gn_ref, n - 10)
            target[pl.ds(group * 64 + start + t, SUB, stride=SUB), :] = value

        def from_packed(ref):
            for t in range(2):
                for n in range(25):
                    put(n, t, ref[(t * 25 + n) * SUB : (t * 25 + n + 1) * SUB, :])

        in_lower = j < info_ref[0]
        in_middle = jnp.logical_not(in_lower) & (j < info_ref[1])

        @pl.when(in_lower)
        def _():
            from_packed(lower_ref)

        @pl.when(in_middle)
        def _():
            slot = jnp.clip(info_ref[3] + j, 0, 3)
            for t in range(2):
                for n in range(25):
                    source, group = (c_ref, n) if n < 10 else (g_ref, n - 10)
                    put(n, t, source[pl.ds(group * 64 + 2 * slot + t, SUB, stride=SUB), :])

        @pl.when(jnp.logical_not(in_lower | in_middle))
        def _():
            from_packed(upper_ref)

        return carry

    lax.fori_loop(0, 3, fill, 0)

    def line_row(axis, place, pos):
        return ((axis * FIELDS + place) * 24 + pos) * SUB

    def put_line(axis, field, pos, value):
        row = line_row(axis, ORDER[axis].index(field), pos)
        line_ref[row : row + SUB, :] = value

    for x in range(EDGE):
        got = [cn_ref[f * PLANE + x * SUB : f * PLANE + (x + 1) * SUB, :] for f in range(FIELDS)]
        for f, value in enumerate(primitives(*got)):
            put_line(0, f, 4 + x, value)
    for f in range(FIELDS):
        row = line_row(0, f, 4)
        rows = [line_ref[row + x * SUB : row + (x + 1) * SUB, :] for x in range(EDGE)]
        for axis, turned in ((1, swap_xy(rows)), (2, swap_xz(rows))):
            for k in range(EDGE):
                put_line(axis, f, 4 + k, turned[k])
        for face in range(6):
            for k in range(4):
                row = face * FACE_ROWS + (f * 4 + k) * SUB
                put_line(face // 2, f, k + 20 * (face % 2), gn_ref[row : row + SUB, :])

    def slopes(axis, carry):
        def line(place, start, stop):
            row = pl.multiple_of((axis * FIELDS + place) * 24 * SUB + start * SUB, SUB)
            return line_ref[pl.ds(row, (stop - start) * SUB), :].reshape(stop - start, SUB, LANES)

        p = line(4, 0, 24)
        jump = jnp.abs(p[3:23] - p[1:21])
        flat = jnp.clip(1.0 - 2.0 * jump / (p[4:24] + p[0:20]), 0.0, 1.0)
        weight = 0.5 * jnp.minimum(jnp.minimum(flat[0:18], flat[1:19]), flat[2:20])
        for place in range(FIELDS):
            w = line(place, 2, 22)
            diff = w[1:20] - w[0:19]
            back, ahead = diff[0:18], diff[1:19]
            mean = 0.5 * (back + ahead)
            twice = diff + diff
            back2, ahead2 = twice[0:18], twice[1:19]
            rise = jnp.maximum(jnp.minimum(mean, jnp.minimum(back2, ahead2)), 0.0)
            fall = jnp.minimum(jnp.maximum(mean, jnp.maximum(back2, ahead2)), 0.0)
            shift = weight * (rise + fall)
            centre = w[1:19]
            left = centre + shift
            right = centre - shift
            row = pl.ds(
                pl.multiple_of((place * 3 + axis) * FACES * SUB, SUB), FACES * SUB
            )
            left_ref[row, :] = left[0:17].reshape(FACES * SUB, LANES)
            right_ref[row, :] = right[1:18].reshape(FACES * SUB, LANES)
        return carry

    lax.fori_loop(0, 3, slopes, 0)

    def flux(step, carry):
        def load(ref, place):
            row = pl.multiple_of((place * 3 * FACES + step * FACE_CHUNK) * SUB, SUB)
            return ref[pl.ds(row, FACE_CHUNK * SUB), :]

        rho_l, u_l, v_l, w_l, p_l = [load(left_ref, k) for k in range(FIELDS)]
        rho_r, u_r, v_r, w_r, p_r = [load(right_ref, k) for k in range(FIELDS)]
        ratio_l = p_l / rho_l
        ratio_r = p_r / rho_r
        c_l = jnp.sqrt(1.4 * ratio_l)
        c_r = jnp.sqrt(1.4 * ratio_r)
        s_l = jnp.minimum(u_l - c_l, u_r - c_r)
        s_r = jnp.maximum(u_l + c_l, u_r + c_r)
        m_l = rho_l * (s_l - u_l)
        m_r = rho_r * (s_r - u_r)
        mid = (p_r - p_l + m_l * u_l - m_r * u_r) / (m_l - m_r)
        use_left = (s_l >= 0.0) | (mid >= 0.0)

        def pick(a, b):
            return jnp.where(use_left, a, b)

        rho, u, v, w, p = (
            pick(rho_l, rho_r),
            pick(u_l, u_r),
            pick(v_l, v_r),
            pick(w_l, w_r),
            pick(p_l, p_r),
        )
        ratio, mass = pick(ratio_l, ratio_r), pick(m_l, m_r)
        wave = pick(jnp.minimum(s_l, 0.0), jnp.maximum(s_r, 0.0))
        starred = wave != 0.0
        scale = jnp.where(starred, wave / jnp.where(starred, wave - mid, 1.0), 0.0)
        f_mass = rho * (u - wave) + scale * mass
        push = scale * (mid - u)
        energy = 2.5 * ratio + 0.5 * (u * u + v * v + w * w)
        values = (
            f_mass,
            u * f_mass + push * mass + p,
            v * f_mass,
            w * f_mass,
            energy * f_mass + p * u + push * (mid * mass + p),
        )
        for place, value in enumerate(values):
            row = pl.multiple_of((place * 3 * FACES + step * FACE_CHUNK) * SUB, SUB)
            flux_ref[pl.ds(row, FACE_CHUNK * SUB), :] = value
        return carry

    lax.fori_loop(0, 3 * FACES // FACE_CHUNK, flux, 0)

    sub = iota(0)
    scale = jnp.zeros((SUB, LANES), jnp.float32)
    filled = (sub >> 1) < info_ref[2]
    for j in range(3):
        level = info_ref[4 + j]
        step = jnp.where(level == 0, 0.02, jnp.where(level == 1, 0.04, 0.08)).astype(jnp.float32)
        scale = jnp.where((sub >> 1) == j, step, scale)

    def change(axis, field):
        base = (ORDER[axis].index(field) * 3 + axis) * FACES * SUB
        rows = [flux_ref[base + k * SUB : base + (k + 1) * SUB, :] for k in range(FACES)]
        return [rows[k + 1] - rows[k] for k in range(EDGE)]

    for f in range(FIELDS):
        along_x = change(0, f)
        along_y = swap_xy(change(1, f))
        along_z = swap_xz(change(2, f))
        for x in range(EDGE):
            place = slice(f * PLANE + x * SUB, f * PLANE + (x + 1) * SUB)
            total = along_x[x] + along_y[x] + along_z[x]
            cn_ref[place, :] = jnp.where(filled, cn_ref[place, :] - scale * total, 0.0)
    for j in range(3):
        for k in range(2 * EDGE):
            x, t = k // 2, k % 2
            out_ref[j, :, k * LANES : (k + 1) * LANES] = cn_ref[
                pl.ds(x * SUB + 2 * j + t, FIELDS, stride=PLANE), :
            ]


def shift_by(value, axis, step):
    count = 1
    for name in (axis,) if isinstance(axis, str) else axis:
        count *= lax.axis_size(name)
    return lax.ppermute(value, axis, [(i, (i + step) % count) for i in range(count)])


def rows_of(count):
    return jax.ShapeDtypeStruct((count, LANES), jnp.float32)


def local(conserved, old_owner, new_owner, box_level, face_source, coarse_part):
    vmem = pl.BlockSpec(memory_space=pltpu.VMEM)
    smem = pl.BlockSpec(memory_space=pltpu.SMEM)
    params = pltpu.CompilerParams(vmem_limit_bytes=VMEM_LIMIT)
    cells, *sent = pl.pallas_call(
        layers_kernel,
        out_shape=[rows_of(FIELDS * PLANE)] + [rows_of(FACE_ROWS)] * 6,
        in_specs=[vmem],
        out_specs=[vmem] * 7,
        scratch_shapes=[pltpu.VMEM((FIELDS * PLANE, LANES), jnp.float32)],
        compiler_params=params,
        name="layers",
    )(conserved)
    got = []
    for axis, name in enumerate(AXES):
        got.append(shift_by(sent[2 * axis + 1], name, 1))
        got.append(shift_by(sent[2 * axis], name, -1))
    info, ghosts, upward, downward = pl.pallas_call(
        ghosts_kernel,
        out_shape=[
            jax.ShapeDtypeStruct((8,), jnp.int32),
            rows_of(6 * FACE_ROWS),
            rows_of(50 * SUB),
            rows_of(50 * SUB),
        ],
        in_specs=[smem] * 5 + [vmem] * 13,
        out_specs=[smem] + [vmem] * 3,
        compiler_params=params,
        name="ghosts",
    )(old_owner, new_owner, box_level, face_source, coarse_part, cells, *sent, *got)
    from_lower = shift_by(upward, AXES, 1)
    from_upper = shift_by(downward, AXES, -1)
    return pl.pallas_call(
        advance_kernel,
        out_shape=jax.ShapeDtypeStruct((3, FIELDS, EDGE**3), jnp.float32),
        in_specs=[smem] + [vmem] * 4,
        out_specs=vmem,
        scratch_shapes=[
            pltpu.VMEM((FIELDS * PLANE, LANES), jnp.float32),
            pltpu.VMEM((6 * FACE_ROWS, LANES), jnp.float32),
            pltpu.VMEM((3 * FIELDS * 24 * SUB, LANES), jnp.float32),
            pltpu.VMEM((3 * FIELDS * FACES * SUB, LANES), jnp.float32),
            pltpu.VMEM((3 * FIELDS * FACES * SUB, LANES), jnp.float32),
            pltpu.VMEM((3 * FIELDS * FACES * SUB, LANES), jnp.float32),
        ],
        compiler_params=params,
        name="advance",
    )(info, cells, ghosts, from_lower, from_upper)


def solution(mesh):
    return jax.shard_map(
        local,
        mesh=mesh,
        in_specs=(P(AXES, None, None), P(), P(), P(), P(AXES, None), P(AXES, None)),
        out_specs=P(AXES, None, None),
        check_vma=False,
    )
```

```python
import jax
import jax.numpy as jnp
from jax import lax
from jax.experimental import pallas as pl
from jax.experimental.pallas import tpu as pltpu
from jax.sharding import PartitionSpec as P

EDGE = 16
FIELDS = 5
LANES = 128
SUB = 8
SLOTS = 4
CELLS = FIELDS * EDGE
AXES = ("gx", "gy", "gz")
ORDER = ((0, 1, 2, 3, 4), (0, 2, 1, 3, 4), (0, 3, 1, 2, 4))
FACE_TILES = 12
INNER = 9
OUTER = 4
NEAR = 6
FACE_CHUNK = 3
PACKED = 2 * CELLS // SUB
VMEM_LIMIT = 48 * 1024 * 1024


def iota(axis):
    return lax.broadcasted_iota(jnp.int32, (SUB, LANES), axis)


def rows(tile, count=1):
    start = tile * SUB
    if not isinstance(start, int):
        start = pl.multiple_of(start, SUB)
    return pl.ds(start, count * SUB)


def get(ref, tile, count):
    return ref[rows(tile, count), :].reshape(count, SUB, LANES)


def put(ref, tile, value):
    count = value.shape[0]
    ref[rows(tile, count), :] = value.reshape(count * SUB, LANES)


def swap_bit(tiles, bit, axis, step):
    size = (SUB, LANES)[axis]
    low = (iota(axis) & step) == 0
    out = list(tiles)
    for i in range(len(tiles)):
        if i & bit:
            continue
        j = i | bit
        a, b = tiles[i], tiles[j]
        out[i] = jnp.where(low, a, pltpu.roll(b, step, axis))
        out[j] = jnp.where(low, pltpu.roll(a, size - step, axis), b)
    return out


def swap_xy(tiles):
    tiles = swap_bit(tiles, 8, 0, 4)
    for bit, step in ((4, 64), (2, 32), (1, 16)):
        tiles = swap_bit(tiles, bit, 1, step)
    return tiles


def swap_xz(tiles):
    for bit, step in ((8, 8), (4, 4), (2, 2), (1, 1)):
        tiles = swap_bit(tiles, bit, 1, step)
    return tiles


def primitives(rho, mx, my, mz, energy):
    inv = 1.0 / rho
    u, v, w = mx * inv, my * inv, mz * inv
    p = 0.4 * (energy - 0.5 * rho * (u * u + v * v + w * w))
    return rho, u, v, w, p


def face_tile(field):
    return 2 * field


def layers_kernel(c_ref, sx0, sx1, sy0, sy1, sz0, sz1, w_ref):
    for x in range(EDGE):
        got = [c_ref[rows(f * EDGE + x), :] for f in range(FIELDS)]
        for f, value in enumerate(primitives(*got)):
            w_ref[rows(f * EDGE + x), :] = value

    def send(f, depth):
        tiles = [w_ref[rows(f * EDGE + x), :] for x in range(EDGE)]
        turned = (swap_xz(tiles), swap_xy(tiles), tiles)
        for got, low, high in zip(turned, (sz0, sy0, sx0), (sz1, sy1, sx1)):
            for r in range(depth):
                low[rows(face_tile(f) + r), :] = got[r]
                high[rows(face_tile(f) + r), :] = got[EDGE - depth + r]

    def field(f, carry):
        send(f, 2)
        return carry

    lax.fori_loop(0, FIELDS - 1, field, 0)
    send(FIELDS - 1, 4)


def device_position():
    place = lax.axis_index(AXES[0])
    for axis in AXES[1:]:
        place = place * lax.axis_size(axis) + lax.axis_index(axis)
    return place


def find_boxes(old_ref, new_ref):
    boxes = old_ref.shape[0]
    place = device_position()

    def halve(_, ends):
        low, high = ends
        middle = (low + high) // 2
        below = old_ref[jnp.minimum(middle, boxes - 1)] < place
        open_ends = low < high
        return (
            jnp.where(open_ends & below, middle + 1, low),
            jnp.where(open_ends & jnp.logical_not(below), middle, high),
        )

    low, _ = lax.fori_loop(0, boxes.bit_length(), halve, (jnp.int32(0), jnp.int32(boxes)))
    count = jnp.int32(0)
    for k in range(SLOTS):
        at = low + k
        mine = (at < boxes) & (old_ref[jnp.minimum(at, boxes - 1)] == place)
        count = count + mine.astype(jnp.int32)
    high = low + count
    before = jnp.maximum(low - 1, 0)
    after = jnp.minimum(high, boxes - 1)
    up_in = ((low > 0) & (new_ref[before] == place)).astype(jnp.int32)
    down_in = ((high < boxes) & (new_ref[after] == place)).astype(jnp.int32)
    down_out = (new_ref[low] == place - 1).astype(jnp.int32)
    up_out = (new_ref[high - 1] == place + 1).astype(jnp.int32)
    return low, count, up_in, down_in, down_out, up_out


def by_slot(values):
    slot = iota(0) & 3
    out = jnp.full((SUB, LANES), values[0])
    for b in range(1, SLOTS):
        out = jnp.where(slot == b, values[b], out)
    return out


def limited(p, fields):
    n = p.shape[0] - 6
    jump = jnp.abs(p[3 : n + 5] - p[1 : n + 3])
    flat = jnp.clip(1.0 - 2.0 * jump / (p[4 : n + 6] + p[0 : n + 2]), 0.0, 1.0)
    weight = 0.5 * jnp.minimum(jnp.minimum(flat[0:n], flat[1 : n + 1]), flat[2 : n + 2])
    left, right = [], []
    for w in fields:
        diff = w[1 : n + 2] - w[0 : n + 1]
        back, ahead = diff[0:n], diff[1 : n + 1]
        mean = 0.5 * (back + ahead)
        twice = diff + diff
        back2, ahead2 = twice[0:n], twice[1 : n + 1]
        rise = jnp.maximum(jnp.minimum(mean, jnp.minimum(back2, ahead2)), 0.0)
        fall = jnp.minimum(jnp.maximum(mean, jnp.maximum(back2, ahead2)), 0.0)
        shift = weight * (rise + fall)
        left.append(w[1 : n + 1] + shift)
        right.append(w[1 : n + 1] - shift)
    return left, right


def hllc(left, right):
    rho_l, u_l, v_l, w_l, p_l = left
    rho_r, u_r, v_r, w_r, p_r = right
    ratio_l = p_l / rho_l
    ratio_r = p_r / rho_r
    c_l = jnp.sqrt(1.4 * ratio_l)
    c_r = jnp.sqrt(1.4 * ratio_r)
    s_l = jnp.minimum(u_l - c_l, u_r - c_r)
    s_r = jnp.maximum(u_l + c_l, u_r + c_r)
    m_l = rho_l * (s_l - u_l)
    m_r = rho_r * (s_r - u_r)
    mid = (p_r - p_l + m_l * u_l - m_r * u_r) / (m_l - m_r)
    use_left = (s_l >= 0.0) | (mid >= 0.0)

    def pick(a, b):
        return jnp.where(use_left, a, b)

    rho, u, v, w, p = (
        pick(rho_l, rho_r),
        pick(u_l, u_r),
        pick(v_l, v_r),
        pick(w_l, w_r),
        pick(p_l, p_r),
    )
    ratio, mass = pick(ratio_l, ratio_r), pick(m_l, m_r)
    wave = pick(jnp.minimum(s_l, 0.0), jnp.maximum(s_r, 0.0))
    starred = wave != 0.0
    scale = jnp.where(starred, wave / jnp.where(starred, wave - mid, 1.0), 0.0)
    f_mass = rho * (u - wave) + scale * mass
    push = scale * (mid - u)
    energy = 2.5 * ratio + 0.5 * (u * u + v * v + w * w)
    return (
        f_mass,
        u * f_mass + push * mass + p,
        v * f_mass,
        w * f_mass,
        energy * f_mass + p * u + push * (mid * mass + p),
    )


def inner_kernel(
    old_ref,
    new_ref,
    level_ref,
    source_ref,
    coarse_ref,
    c_ref,
    info_ref,
    index_ref,
    scale_ref,
    near_ref,
    flux_ref,
    edge_ref,
    line_ref,
    left_ref,
    right_ref,
):
    low, count, up_in, down_in, down_out, up_out = find_boxes(old_ref, new_ref)
    boxes = old_ref.shape[0]
    staying = count - down_out - up_out
    info_ref[0] = up_in
    info_ref[1] = up_in + staying
    info_ref[2] = up_in + staying + down_in
    info_ref[3] = down_out - up_in
    info_ref[4] = count - 1
    steps = []
    for b in range(SLOTS):
        level = level_ref[jnp.minimum(low + b, boxes - 1)]
        steps.append(
            jnp.where(level == 0, 0.02, jnp.where(level == 1, 0.04, 0.08)).astype(jnp.float32)
        )
    scale_ref[...] = by_slot(steps)
    half, lane = iota(0) >> 2, iota(1)
    for face in range(6):
        slot_rows = by_slot([source_ref[b, face] for b in range(SLOTS)])
        codes = by_slot([coarse_ref[b, face] for b in range(SLOTS)])
        is_coarse = codes > 0
        quadrant = codes - 1
        first, second = (quadrant >> 1) & 1, quadrant & 1
        if face // 2 == 2:
            first, second = second, first
        index_ref[rows(3 * face), :] = (slot_rows & 3) + 4 * jnp.where(is_coarse, first, half)
        index_ref[rows(3 * face + 1), :] = jnp.where(
            is_coarse,
            (half * 4 + (lane >> 5)) * EDGE + second * 8 + ((lane & 15) >> 1),
            lane,
        )
        index_ref[rows(3 * face + 2), :] = (slot_rows >> 2) + 2 * is_coarse.astype(jnp.int32)

    def line_tile(axis, field, pos):
        return (axis * FIELDS + ORDER[axis].index(field)) * EDGE + pos

    for x in range(EDGE):
        got = [c_ref[rows(f * EDGE + x), :] for f in range(FIELDS)]
        for f, value in enumerate(primitives(*got)):
            line_ref[rows(line_tile(0, f, x)), :] = value
    for f in range(FIELDS):
        tiles = [line_ref[rows(line_tile(0, f, x)), :] for x in range(EDGE)]
        for axis, turned in ((0, tiles), (1, swap_xy(tiles)), (2, swap_xz(tiles))):
            for k in range(EDGE):
                if axis > 0:
                    line_ref[rows(line_tile(axis, f, k)), :] = turned[k]
            place = ORDER[axis].index(f)
            for k in range(NEAR):
                near_ref[rows(((axis * 2) * FIELDS + place) * NEAR + k), :] = turned[k]
                near_ref[rows(((axis * 2 + 1) * FIELDS + place) * NEAR + k), :] = turned[
                    EDGE - NEAR + k
                ]

    def slopes(axis, carry):
        base = axis * FIELDS
        p = get(line_ref, (base + 4) * EDGE, EDGE)
        fields = [get(line_ref, (base + k) * EDGE + 2, INNER + 3) for k in range(FIELDS)]
        left, right = limited(p, fields)
        for k in range(FIELDS):
            put(left_ref, (k * 3 + axis) * INNER, left[k][0:INNER])
            put(right_ref, (k * 3 + axis) * INNER, right[k][1 : INNER + 1])
            put(edge_ref, (axis * 2) * FIELDS + k, right[k][0:1])
            put(edge_ref, (axis * 2 + 1) * FIELDS + k, left[k][INNER : INNER + 1])
        return carry

    lax.fori_loop(0, 3, slopes, 0)

    def flux(step, carry):
        def load(ref):
            return [get(ref, k * 3 * INNER + step * FACE_CHUNK, FACE_CHUNK) for k in range(FIELDS)]

        for k, value in enumerate(hllc(load(left_ref), load(right_ref))):
            put(flux_ref, k * 3 * INNER + step * FACE_CHUNK, value)
        return carry

    lax.fori_loop(0, 3 * INNER // FACE_CHUNK, flux, 0)


def outer_kernel(*refs):
    info_ref, c_ref = refs[0:2]
    own, got = refs[2:8], refs[8:14]
    index_ref, scale_ref, near_ref, inner_ref, edge_ref = refs[14:19]
    new_ref, up_ref, down_ref = refs[19:22]
    ghost_ref, flux_ref = refs[22:24]

    for face in range(6):
        axis, side = face // 2, face % 2
        from_row = index_ref[rows(3 * face), :]
        from_lane = index_ref[rows(3 * face + 1), :]
        flags = index_ref[rows(3 * face + 2), :]
        is_own = (flags & 1) == 1
        is_coarse = flags >= 2
        mine, theirs = own[2 * axis + 1 - side], got[face]
        for f in range(FIELDS):
            depth = 4 if f == 4 else 2
            picked = []
            for r in range(depth):
                place = rows(face_tile(f) + r)
                picked.append(
                    jnp.where(
                        is_own,
                        jnp.take_along_axis(mine[place, :], from_row, axis=0),
                        jnp.take_along_axis(theirs[place, :], from_row, axis=0),
                    )
                )
            for k in range(depth):
                source = picked[(depth // 2 if side == 0 else 0) + k // 2]
                chosen = jnp.where(is_coarse, source, picked[k])
                row = face * FACE_TILES + face_tile(ORDER[axis].index(f)) + k
                ghost_ref[rows(row), :] = jnp.take_along_axis(chosen, from_lane, axis=1)

    def edges(axis, carry):
        for side in range(2):
            face = axis * 2 + side

            def line(k):
                ghost = get(ghost_ref, face * FACE_TILES + face_tile(k), 4 if k == 4 else 2)
                start = (face * FIELDS + k) * NEAR
                if k == 4:
                    near = get(near_ref, start, NEAR)
                else:
                    near = get(near_ref, start + 2 * side, 4)
                pieces = (ghost, near) if side == 0 else (near, ghost)
                return jnp.concatenate(pieces, axis=0)

            p = line(4)
            fields = [line(k) for k in range(4)] + [p[2:8]]
            left, right = limited(p, fields)
            edge = [get(edge_ref, face * FIELDS + k, 1) for k in range(FIELDS)]
            if side == 0:
                right = [jnp.concatenate([a[1:], b], axis=0) for a, b in zip(right, edge)]
            else:
                left = [jnp.concatenate([b, a[:-1]], axis=0) for a, b in zip(left, edge)]
            for k, value in enumerate(hllc(left, right)):
                put(flux_ref, (face * FIELDS + k) * OUTER, value)
        return carry

    lax.fori_loop(0, 3, edges, 0)

    def change(axis, field):
        place = ORDER[axis].index(field)
        faces = [
            flux_ref[rows((axis * 2 * FIELDS + place) * OUTER + k), :] for k in range(OUTER)
        ]
        faces += [inner_ref[rows((place * 3 + axis) * INNER + k), :] for k in range(INNER)]
        faces += [
            flux_ref[rows(((axis * 2 + 1) * FIELDS + place) * OUTER + k), :] for k in range(OUTER)
        ]
        return [faces[k + 1] - faces[k] for k in range(EDGE)]

    scale = scale_ref[...]
    for f in range(FIELDS):
        along_x = change(0, f)
        along_y = swap_xy(change(1, f))
        along_z = swap_xz(change(2, f))
        for x in range(EDGE):
            total = along_x[x] + along_y[x] + along_z[x]
            place = rows(f * EDGE + x)
            new_ref[place, :] = c_ref[place, :] - scale * total
    for slot, out in ((info_ref[4], up_ref), (0, down_ref)):
        for t in range(2):
            for n in range(CELLS // SUB):
                out[rows(t * (CELLS // SUB) + n), :] = new_ref[
                    pl.ds(n * 64 + 4 * t + slot, SUB, stride=SUB), :
                ]


def place_kernel(info_ref, new_ref, lower_ref, upper_ref, out_ref):
    slot = iota(0) & 3
    first = iota(0) < 4
    stays = (slot >= info_ref[0]) & (slot < info_ref[1])
    from_lower = slot < info_ref[0]
    from_upper = (slot >= info_ref[1]) & (slot < info_ref[2])
    from_row = (iota(0) & 4) + ((slot + info_ref[3]) & 3)
    for f in range(FIELDS):
        for x in range(EDGE):
            n = f * EDGE + x

            def spread(ref):
                a = jnp.broadcast_to(ref[pl.ds(n, 1), :], (SUB, LANES))
                b = jnp.broadcast_to(ref[pl.ds(CELLS + n, 1), :], (SUB, LANES))
                return jnp.where(first, a, b)

            value = jnp.take_along_axis(new_ref[rows(n), :], from_row, axis=0)
            value = jnp.where(stays, value, 0.0)
            value = jnp.where(from_lower, spread(lower_ref), value)
            value = jnp.where(from_upper, spread(upper_ref), value)
            for t in range(2):
                lanes = slice((2 * x + t) * LANES, (2 * x + t + 1) * LANES)
                out_ref[f, :, lanes] = value[4 * t : 4 * t + 3]


def shift_by(value, axis, step):
    count = 1
    for name in (axis,) if isinstance(axis, str) else axis:
        count *= lax.axis_size(name)
    return lax.ppermute(value, axis, [(i, (i + step) % count) for i in range(count)])


def tiles_of(count, dtype=jnp.float32):
    return jax.ShapeDtypeStruct((count * SUB, LANES), dtype)


def scratch(count):
    return pltpu.VMEM((count * SUB, LANES), jnp.float32)


def local(conserved, old_owner, new_owner, box_level, face_source, coarse_part):
    vmem = pl.BlockSpec(memory_space=pltpu.VMEM)
    smem = pl.BlockSpec(memory_space=pltpu.SMEM)
    params = pltpu.CompilerParams(vmem_limit_bytes=VMEM_LIMIT)
    cells = conserved.transpose(1, 0, 2).reshape(FIELDS, SLOTS, 2 * EDGE, LANES)
    cells = cells.transpose(0, 2, 1, 3).reshape(CELLS * SUB, LANES)
    sent = pl.pallas_call(
        layers_kernel,
        out_shape=[tiles_of(FACE_TILES)] * 6,
        in_specs=[vmem],
        out_specs=[vmem] * 6,
        scratch_shapes=[scratch(CELLS)],
        compiler_params=params,
        name="layers",
    )(cells)
    got = [None] * 6
    for axis in (2, 1, 0):
        got[2 * axis] = shift_by(sent[2 * axis + 1], AXES[axis], 1)
        got[2 * axis + 1] = shift_by(sent[2 * axis], AXES[axis], -1)
    info, *inner = pl.pallas_call(
        inner_kernel,
        out_shape=[
            jax.ShapeDtypeStruct((8,), jnp.int32),
            tiles_of(18, jnp.int32),
            tiles_of(1),
            tiles_of(6 * FIELDS * NEAR),
            tiles_of(FIELDS * 3 * INNER),
            tiles_of(6 * FIELDS),
        ],
        in_specs=[smem] * 5 + [vmem],
        out_specs=[smem] + [vmem] * 5,
        scratch_shapes=[
            scratch(3 * CELLS),
            scratch(FIELDS * 3 * INNER),
            scratch(FIELDS * 3 * INNER),
        ],
        compiler_params=params,
        name="inner",
    )(old_owner, new_owner, box_level, face_source, coarse_part, cells)
    updated, upward, downward = pl.pallas_call(
        outer_kernel,
        out_shape=[tiles_of(CELLS), tiles_of(PACKED), tiles_of(PACKED)],
        in_specs=[smem] + [vmem] * 18,
        out_specs=[vmem] * 3,
        scratch_shapes=[scratch(6 * FACE_TILES), scratch(6 * FIELDS * OUTER)],
        compiler_params=params,
        name="outer",
    )(info, cells, *sent, *got, *inner)
    from_lower = shift_by(upward, AXES, 1)
    from_upper = shift_by(downward, AXES, -1)
    out = pl.pallas_call(
        place_kernel,
        out_shape=jax.ShapeDtypeStruct((FIELDS, 3, EDGE**3), jnp.float32),
        in_specs=[smem] + [vmem] * 3,
        out_specs=vmem,
        compiler_params=params,
        name="place",
    )(info, updated, from_lower, from_upper)
    return out.transpose(1, 0, 2)


def solution(mesh):
    return jax.shard_map(
        local,
        mesh=mesh,
        in_specs=(P(AXES, None, None), P(), P(), P(), P(AXES, None), P(AXES, None)),
        out_specs=P(AXES, None, None),
        check_vma=False,
    )
```

```python
import jax
import jax.numpy as jnp
from jax import lax
from jax.experimental import pallas as pl
from jax.experimental.pallas import tpu as pltpu
from jax.sharding import PartitionSpec as P

EDGE = 16
FIELDS = 5
LANES = 128
SUB = 8
SLOTS = 4
CELLS = FIELDS * EDGE
AXES = ("gx", "gy", "gz")
ORDER = ((0, 1, 2, 3, 4), (0, 2, 1, 3, 4), (0, 3, 1, 2, 4))
FACE_TILES = 12
INNER = 9
OUTER = 4
NEAR = 6
FACE_CHUNK = 3
PACKED = 2 * CELLS // SUB
VMEM_LIMIT = 48 * 1024 * 1024


def iota(axis):
    return lax.broadcasted_iota(jnp.int32, (SUB, LANES), axis)


def rows(tile, count=1):
    start = tile * SUB
    if not isinstance(start, int):
        start = pl.multiple_of(start, SUB)
    return pl.ds(start, count * SUB)


def get(ref, tile, count):
    return ref[rows(tile, count), :].reshape(count, SUB, LANES)


def put(ref, tile, value):
    count = value.shape[0]
    ref[rows(tile, count), :] = value.reshape(count * SUB, LANES)


def swap_bit(tiles, bit, axis, step):
    low = (iota(axis) & step) == 0
    across = iota(axis) ^ step
    out = list(tiles)
    for i in range(len(tiles)):
        if i & bit:
            continue
        j = i | bit
        a, b = tiles[i], tiles[j]
        moving = jnp.where(low, b, a)
        if 2 * step == (SUB, LANES)[axis]:
            moved = pltpu.roll(moving, step, axis)
        else:
            moved = jnp.take_along_axis(moving, across, axis=axis)
        out[i] = jnp.where(low, a, moved)
        out[j] = jnp.where(low, moved, b)
    return out


def swap_xy(tiles):
    tiles = swap_bit(tiles, 8, 0, 4)
    for bit, step in ((4, 64), (2, 32), (1, 16)):
        tiles = swap_bit(tiles, bit, 1, step)
    return tiles


def to_z(field_tiles, turn_ref):
    turn_ref[...] = field_tiles.T
    return [turn_ref[pl.ds(z, SUB, stride=EDGE), :] for z in range(EDGE)]


def from_z(tiles, turn_ref):
    for z in range(EDGE):
        turn_ref[pl.ds(z, SUB, stride=EDGE), :] = tiles[z]
    whole = turn_ref[...].T
    return [whole[k * SUB : (k + 1) * SUB] for k in range(EDGE)]


def primitives(rho, mx, my, mz, energy):
    inv = 1.0 / rho
    u, v, w = mx * inv, my * inv, mz * inv
    p = 0.4 * (energy - 0.5 * rho * (u * u + v * v + w * w))
    return rho, u, v, w, p


def face_tile(field):
    return 2 * field


def layers_kernel(c_ref, sx0, sx1, sy0, sy1, sz0, sz1, w_ref, turn_ref):
    for x in range(EDGE):
        got = [c_ref[rows(f * EDGE + x), :] for f in range(FIELDS)]
        for f, value in enumerate(primitives(*got)):
            w_ref[rows(f * EDGE + x), :] = value
    for f in range(FIELDS):
        depth = 4 if f == 4 else 2
        tiles = [w_ref[rows(f * EDGE + x), :] for x in range(EDGE)]
        turned_z = to_z(w_ref[rows(f * EDGE, EDGE), :], turn_ref.at[rows(f * EDGE, EDGE)])
        turned = (turned_z, swap_xy(tiles), tiles)
        for got, low, high in zip(turned, (sz0, sy0, sx0), (sz1, sy1, sx1)):
            for r in range(depth):
                low[rows(face_tile(f) + r), :] = got[r]
                high[rows(face_tile(f) + r), :] = got[EDGE - depth + r]


def device_position():
    place = lax.axis_index(AXES[0])
    for axis in AXES[1:]:
        place = place * lax.axis_size(axis) + lax.axis_index(axis)
    return place


def find_boxes(old_ref, new_ref):
    boxes = old_ref.shape[0]
    place = device_position()

    def halve(_, ends):
        low, high = ends
        middle = (low + high) // 2
        below = old_ref[jnp.minimum(middle, boxes - 1)] < place
        open_ends = low < high
        return (
            jnp.where(open_ends & below, middle + 1, low),
            jnp.where(open_ends & jnp.logical_not(below), middle, high),
        )

    low, _ = lax.fori_loop(0, boxes.bit_length(), halve, (jnp.int32(0), jnp.int32(boxes)))
    count = jnp.int32(0)
    for k in range(SLOTS):
        at = low + k
        mine = (at < boxes) & (old_ref[jnp.minimum(at, boxes - 1)] == place)
        count = count + mine.astype(jnp.int32)
    high = low + count
    before = jnp.maximum(low - 1, 0)
    after = jnp.minimum(high, boxes - 1)
    up_in = ((low > 0) & (new_ref[before] == place)).astype(jnp.int32)
    down_in = ((high < boxes) & (new_ref[after] == place)).astype(jnp.int32)
    down_out = (new_ref[low] == place - 1).astype(jnp.int32)
    up_out = (new_ref[high - 1] == place + 1).astype(jnp.int32)
    return low, count, up_in, down_in, down_out, up_out


def by_slot(values, axis=0):
    slot = iota(axis) & 3
    out = jnp.full((SUB, LANES), values[0])
    for b in range(1, SLOTS):
        out = jnp.where(slot == b, values[b], out)
    return out


def limited(p, fields):
    n = p.shape[0] - 6
    jump = jnp.abs(p[3 : n + 5] - p[1 : n + 3])
    flat = jnp.clip(1.0 - 2.0 * jump / (p[4 : n + 6] + p[0 : n + 2]), 0.0, 1.0)
    weight = 0.5 * jnp.minimum(jnp.minimum(flat[0:n], flat[1 : n + 1]), flat[2 : n + 2])
    left, right = [], []
    for w in fields:
        diff = w[1 : n + 2] - w[0 : n + 1]
        back, ahead = diff[0:n], diff[1 : n + 1]
        mean = 0.5 * (back + ahead)
        twice = diff + diff
        back2, ahead2 = twice[0:n], twice[1 : n + 1]
        rise = jnp.maximum(jnp.minimum(mean, jnp.minimum(back2, ahead2)), 0.0)
        fall = jnp.minimum(jnp.maximum(mean, jnp.maximum(back2, ahead2)), 0.0)
        shift = weight * (rise + fall)
        left.append(w[1 : n + 1] + shift)
        right.append(w[1 : n + 1] - shift)
    return left, right


def hllc(left, right):
    rho_l, u_l, v_l, w_l, p_l = left
    rho_r, u_r, v_r, w_r, p_r = right
    ratio_l = p_l / rho_l
    ratio_r = p_r / rho_r
    c_l = jnp.sqrt(1.4 * ratio_l)
    c_r = jnp.sqrt(1.4 * ratio_r)
    s_l = jnp.minimum(u_l - c_l, u_r - c_r)
    s_r = jnp.maximum(u_l + c_l, u_r + c_r)
    m_l = rho_l * (s_l - u_l)
    m_r = rho_r * (s_r - u_r)
    mid = (p_r - p_l + m_l * u_l - m_r * u_r) / (m_l - m_r)
    use_left = (s_l >= 0.0) | (mid >= 0.0)

    def pick(a, b):
        return jnp.where(use_left, a, b)

    rho, u, v, w, p = (
        pick(rho_l, rho_r),
        pick(u_l, u_r),
        pick(v_l, v_r),
        pick(w_l, w_r),
        pick(p_l, p_r),
    )
    ratio, mass = pick(ratio_l, ratio_r), pick(m_l, m_r)
    wave = pick(jnp.minimum(s_l, 0.0), jnp.maximum(s_r, 0.0))
    starred = wave != 0.0
    scale = jnp.where(starred, wave / jnp.where(starred, wave - mid, 1.0), 0.0)
    f_mass = rho * (u - wave) + scale * mass
    push = scale * (mid - u)
    energy = 2.5 * ratio + 0.5 * (u * u + v * v + w * w)
    return (
        f_mass,
        u * f_mass + push * mass + p,
        v * f_mass,
        w * f_mass,
        energy * f_mass + p * u + push * (mid * mass + p),
    )


def inner_kernel(
    old_ref,
    new_ref,
    level_ref,
    source_ref,
    coarse_ref,
    c_ref,
    info_ref,
    index_ref,
    scale_ref,
    near_ref,
    flux_ref,
    edge_ref,
    line_ref,
    left_ref,
    right_ref,
    turn_ref,
):
    low, count, up_in, down_in, down_out, up_out = find_boxes(old_ref, new_ref)
    boxes = old_ref.shape[0]
    staying = count - down_out - up_out
    info_ref[0] = up_in
    info_ref[1] = up_in + staying
    info_ref[2] = up_in + staying + down_in
    info_ref[3] = down_out - up_in
    info_ref[4] = count - 1
    steps = []
    for b in range(SLOTS):
        level = level_ref[jnp.minimum(low + b, boxes - 1)]
        steps.append(
            jnp.where(level == 0, 0.02, jnp.where(level == 1, 0.04, 0.08)).astype(jnp.float32)
        )
    scale_ref[...] = by_slot(steps)
    sub, lane = iota(0), iota(1)
    for face in range(6):
        along = 1 if face // 2 == 2 else 0
        source = by_slot([source_ref[b, face] for b in range(SLOTS)], along)
        codes = by_slot([coarse_ref[b, face] for b in range(SLOTS)], along)
        is_coarse = codes > 0
        quadrant = codes - 1
        first, second = (quadrant >> 1) & 1, quadrant & 1
        if along == 0:
            half = sub >> 2
            from_row = (source & 3) + 4 * jnp.where(is_coarse, first, half)
            near = (half * 4 + (lane >> 5)) * EDGE + second * 8 + ((lane & 15) >> 1)
            from_lane = jnp.where(is_coarse, near, lane)
        else:
            half = (lane >> 2) & 1
            from_row = jnp.where(is_coarse, half * 4 + (sub >> 1), sub)
            near = (first * 8 + (lane >> 4)) * 8 + second * 4
            from_lane = (source & 3) + jnp.where(is_coarse, near, lane & 124)
        index_ref[rows(3 * face), :] = from_row
        index_ref[rows(3 * face + 1), :] = from_lane
        index_ref[rows(3 * face + 2), :] = (source >> 2) + 2 * is_coarse.astype(jnp.int32)

    def line_tile(axis, field, pos):
        return (axis * FIELDS + ORDER[axis].index(field)) * EDGE + pos

    for x in range(EDGE):
        got = [c_ref[rows(f * EDGE + x), :] for f in range(FIELDS)]
        for f, value in enumerate(primitives(*got)):
            line_ref[rows(line_tile(0, f, x)), :] = value
    def near(axis, f, tiles):
        place = ORDER[axis].index(f)
        for k in range(EDGE):
            if axis > 0:
                line_ref[rows(line_tile(axis, f, k)), :] = tiles[k]
        for k in range(NEAR):
            near_ref[rows(((axis * 2) * FIELDS + place) * NEAR + k), :] = tiles[k]
            near_ref[rows(((axis * 2 + 1) * FIELDS + place) * NEAR + k), :] = tiles[
                EDGE - NEAR + k
            ]

    for f in range(FIELDS):
        tiles = [line_ref[rows(line_tile(0, f, x)), :] for x in range(EDGE)]
        near(0, f, tiles)
        whole = line_ref[rows(line_tile(0, f, 0), EDGE), :]
        near(2, f, to_z(whole, turn_ref.at[rows(f * EDGE, EDGE)]))
        near(1, f, swap_xy(tiles))

    def slopes(axis, carry):
        base = axis * FIELDS
        p = get(line_ref, (base + 4) * EDGE, EDGE)
        fields = [get(line_ref, (base + k) * EDGE + 2, INNER + 3) for k in range(FIELDS)]
        left, right = limited(p, fields)
        for k in range(FIELDS):
            put(left_ref, (k * 3 + axis) * INNER, left[k][0:INNER])
            put(right_ref, (k * 3 + axis) * INNER, right[k][1 : INNER + 1])
            put(edge_ref, (axis * 2) * FIELDS + k, right[k][0:1])
            put(edge_ref, (axis * 2 + 1) * FIELDS + k, left[k][INNER : INNER + 1])
        return carry

    lax.fori_loop(0, 3, slopes, 0)

    def flux(step, carry):
        def load(ref):
            return [get(ref, k * 3 * INNER + step * FACE_CHUNK, FACE_CHUNK) for k in range(FIELDS)]

        for k, value in enumerate(hllc(load(left_ref), load(right_ref))):
            put(flux_ref, k * 3 * INNER + step * FACE_CHUNK, value)
        return carry

    lax.fori_loop(0, 3 * INNER // FACE_CHUNK, flux, 0)


def outer_kernel(*refs):
    info_ref, c_ref = refs[0:2]
    own, got = refs[2:8], refs[8:14]
    index_ref, scale_ref, near_ref, inner_ref, edge_ref = refs[14:19]
    new_ref, up_ref, down_ref = refs[19:22]
    ghost_ref, flux_ref, turn_ref = refs[22:25]

    for face in range(6):
        axis, side = face // 2, face % 2
        from_row = index_ref[rows(3 * face), :]
        from_lane = index_ref[rows(3 * face + 1), :]
        flags = index_ref[rows(3 * face + 2), :]
        is_own = (flags & 1) == 1
        is_coarse = flags >= 2
        mine, theirs = own[2 * axis + 1 - side], got[face]
        turns = ((from_row, 0), (from_lane, 1))
        before, after = turns if axis < 2 else turns[::-1]
        for f in range(FIELDS):
            depth = 4 if f == 4 else 2
            picked = []
            for r in range(depth):
                place = rows(face_tile(f) + r)
                picked.append(
                    jnp.where(
                        is_own,
                        jnp.take_along_axis(mine[place, :], before[0], axis=before[1]),
                        jnp.take_along_axis(theirs[place, :], before[0], axis=before[1]),
                    )
                )
            for k in range(depth):
                source = picked[(depth // 2 if side == 0 else 0) + k // 2]
                chosen = jnp.where(is_coarse, source, picked[k])
                row = face * FACE_TILES + face_tile(ORDER[axis].index(f)) + k
                ghost_ref[rows(row), :] = jnp.take_along_axis(chosen, after[0], axis=after[1])

    def edges(axis, carry):
        for side in range(2):
            face = axis * 2 + side

            def line(k):
                ghost = get(ghost_ref, face * FACE_TILES + face_tile(k), 4 if k == 4 else 2)
                start = (face * FIELDS + k) * NEAR
                if k == 4:
                    near = get(near_ref, start, NEAR)
                else:
                    near = get(near_ref, start + 2 * side, 4)
                pieces = (ghost, near) if side == 0 else (near, ghost)
                return jnp.concatenate(pieces, axis=0)

            p = line(4)
            fields = [line(k) for k in range(4)] + [p[2:8]]
            left, right = limited(p, fields)
            edge = [get(edge_ref, face * FIELDS + k, 1) for k in range(FIELDS)]
            if side == 0:
                right = [jnp.concatenate([a[1:], b], axis=0) for a, b in zip(right, edge)]
            else:
                left = [jnp.concatenate([b, a[:-1]], axis=0) for a, b in zip(left, edge)]
            for k, value in enumerate(hllc(left, right)):
                put(flux_ref, (face * FIELDS + k) * OUTER, value)
        return carry

    lax.fori_loop(0, 3, edges, 0)

    def change(axis, field):
        place = ORDER[axis].index(field)
        faces = [
            flux_ref[rows((axis * 2 * FIELDS + place) * OUTER + k), :] for k in range(OUTER)
        ]
        faces += [inner_ref[rows((place * 3 + axis) * INNER + k), :] for k in range(INNER)]
        faces += [
            flux_ref[rows(((axis * 2 + 1) * FIELDS + place) * OUTER + k), :] for k in range(OUTER)
        ]
        return [faces[k + 1] - faces[k] for k in range(EDGE)]

    scale = scale_ref[...]
    for f in range(FIELDS):
        along_x = change(0, f)
        along_y = swap_xy(change(1, f))
        along_z = from_z(change(2, f), turn_ref.at[rows(f * EDGE, EDGE)])
        for x in range(EDGE):
            total = along_x[x] + along_y[x] + along_z[x]
            place = rows(f * EDGE + x)
            new_ref[place, :] = c_ref[place, :] - scale * total
    for slot, out in ((info_ref[4], up_ref), (0, down_ref)):
        for t in range(2):
            for n in range(CELLS // SUB):
                out[rows(t * (CELLS // SUB) + n), :] = new_ref[
                    pl.ds(n * 64 + 4 * t + slot, SUB, stride=SUB), :
                ]


def place_kernel(info_ref, new_ref, lower_ref, upper_ref, out_ref):
    slot = iota(0) & 3
    first = iota(0) < 4
    stays = (slot >= info_ref[0]) & (slot < info_ref[1])
    from_lower = slot < info_ref[0]
    from_upper = (slot >= info_ref[1]) & (slot < info_ref[2])
    from_row = (iota(0) & 4) + ((slot + info_ref[3]) & 3)
    for f in range(FIELDS):
        for x in range(EDGE):
            n = f * EDGE + x

            def spread(ref):
                a = jnp.broadcast_to(ref[pl.ds(n, 1), :], (SUB, LANES))
                b = jnp.broadcast_to(ref[pl.ds(CELLS + n, 1), :], (SUB, LANES))
                return jnp.where(first, a, b)

            value = jnp.take_along_axis(new_ref[rows(n), :], from_row, axis=0)
            value = jnp.where(stays, value, 0.0)
            value = jnp.where(from_lower, spread(lower_ref), value)
            value = jnp.where(from_upper, spread(upper_ref), value)
            for t in range(2):
                lanes = slice((2 * x + t) * LANES, (2 * x + t + 1) * LANES)
                out_ref[f, :, lanes] = value[4 * t : 4 * t + 3]


def shift_by(value, axis, step):
    count = 1
    for name in (axis,) if isinstance(axis, str) else axis:
        count *= lax.axis_size(name)
    return lax.ppermute(value, axis, [(i, (i + step) % count) for i in range(count)])


def tiles_of(count, dtype=jnp.float32):
    return jax.ShapeDtypeStruct((count * SUB, LANES), dtype)


def scratch(count):
    return pltpu.VMEM((count * SUB, LANES), jnp.float32)


def local(conserved, old_owner, new_owner, box_level, face_source, coarse_part):
    vmem = pl.BlockSpec(memory_space=pltpu.VMEM)
    smem = pl.BlockSpec(memory_space=pltpu.SMEM)
    params = pltpu.CompilerParams(vmem_limit_bytes=VMEM_LIMIT)
    cells = conserved.transpose(1, 0, 2).reshape(FIELDS, SLOTS, 2 * EDGE, LANES)
    cells = cells.transpose(0, 2, 1, 3).reshape(CELLS * SUB, LANES)
    sent = pl.pallas_call(
        layers_kernel,
        out_shape=[tiles_of(FACE_TILES)] * 6,
        in_specs=[vmem],
        out_specs=[vmem] * 6,
        scratch_shapes=[scratch(CELLS)] * 2,
        compiler_params=params,
        name="layers",
    )(cells)
    got = [None] * 6
    for axis in (2, 1, 0):
        got[2 * axis] = shift_by(sent[2 * axis + 1], AXES[axis], 1)
        got[2 * axis + 1] = shift_by(sent[2 * axis], AXES[axis], -1)
    info, *inner = pl.pallas_call(
        inner_kernel,
        out_shape=[
            jax.ShapeDtypeStruct((8,), jnp.int32),
            tiles_of(18, jnp.int32),
            tiles_of(1),
            tiles_of(6 * FIELDS * NEAR),
            tiles_of(FIELDS * 3 * INNER),
            tiles_of(6 * FIELDS),
        ],
        in_specs=[smem] * 5 + [vmem],
        out_specs=[smem] + [vmem] * 5,
        scratch_shapes=[
            scratch(3 * CELLS),
            scratch(FIELDS * 3 * INNER),
            scratch(FIELDS * 3 * INNER),
            scratch(CELLS),
        ],
        compiler_params=params,
        name="inner",
    )(old_owner, new_owner, box_level, face_source, coarse_part, cells)
    updated, upward, downward = pl.pallas_call(
        outer_kernel,
        out_shape=[tiles_of(CELLS), tiles_of(PACKED), tiles_of(PACKED)],
        in_specs=[smem] + [vmem] * 18,
        out_specs=[vmem] * 3,
        scratch_shapes=[scratch(6 * FACE_TILES), scratch(6 * FIELDS * OUTER), scratch(CELLS)],
        compiler_params=params,
        name="outer",
    )(info, cells, *sent, *got, *inner)
    from_lower = shift_by(upward, AXES, 1)
    from_upper = shift_by(downward, AXES, -1)
    out = pl.pallas_call(
        place_kernel,
        out_shape=jax.ShapeDtypeStruct((FIELDS, 3, EDGE**3), jnp.float32),
        in_specs=[smem] + [vmem] * 3,
        out_specs=vmem,
        compiler_params=params,
        name="place",
    )(info, updated, from_lower, from_upper)
    return out.transpose(1, 0, 2)


def solution(mesh):
    return jax.shard_map(
        local,
        mesh=mesh,
        in_specs=(P(AXES, None, None), P(), P(), P(), P(AXES, None), P(AXES, None)),
        out_specs=P(AXES, None, None),
        check_vma=False,
    )
```

```python
import jax
import jax.numpy as jnp
from jax import lax
from jax.experimental import pallas as pl
from jax.experimental.pallas import tpu as pltpu
from jax.sharding import PartitionSpec as P

EDGE = 16
FIELDS = 5
LANES = 128
SUB = 8
SLOTS = 4
CELLS = FIELDS * EDGE
AXES = ("gx", "gy", "gz")
ORDER = ((0, 1, 2, 3, 4), (0, 2, 1, 3, 4), (0, 3, 1, 2, 4))
FACE_TILES = 12
INNER = 9
OUTER = 4
QUARTER = 4
FACE_CHUNK = 3
PACKED = 2 * CELLS // SUB
VMEM_LIMIT = 48 * 1024 * 1024


def iota(axis):
    return lax.broadcasted_iota(jnp.int32, (SUB, LANES), axis)


def rows(tile, count=1):
    start = tile * SUB
    if not isinstance(start, int):
        start = pl.multiple_of(start, SUB)
    return pl.ds(start, count * SUB)


def get(ref, tile, count):
    return ref[rows(tile, count), :].reshape(count, SUB, LANES)


def put(ref, tile, value):
    count = value.shape[0]
    ref[rows(tile, count), :] = value.reshape(count * SUB, LANES)


def swap_bit(tiles, bit, axis, step):
    low = (iota(axis) & step) == 0
    across = iota(axis) ^ step
    out = list(tiles)
    for i in range(len(tiles)):
        if i & bit:
            continue
        j = i | bit
        a, b = tiles[i], tiles[j]
        moving = jnp.where(low, b, a)
        if 2 * step == (SUB, LANES)[axis]:
            moved = pltpu.roll(moving, step, axis)
        else:
            moved = jnp.take_along_axis(moving, across, axis=axis)
        out[i] = jnp.where(low, a, moved)
        out[j] = jnp.where(low, moved, b)
    return out


def swap_xy(tiles):
    tiles = swap_bit(tiles, 8, 0, 4)
    for bit, step in ((4, 64), (2, 32), (1, 16)):
        tiles = swap_bit(tiles, bit, 1, step)
    return tiles


def z_tile(ref, field, z):
    return ref[pl.ds(field * EDGE * SUB + z, SUB, stride=EDGE), :]


def from_z(tiles, turn_ref):
    for z in range(EDGE):
        turn_ref[pl.ds(z, SUB, stride=EDGE), :] = tiles[z]
    whole = turn_ref[...].T
    return [whole[k * SUB : (k + 1) * SUB] for k in range(EDGE)]


def primitives(rho, mx, my, mz, energy):
    inv = 1.0 / rho
    u, v, w = mx * inv, my * inv, mz * inv
    p = 0.4 * (energy - 0.5 * rho * (u * u + v * v + w * w))
    return rho, u, v, w, p


def face_tile(field):
    return 2 * field


def layers_kernel(c_ref, sx0, sx1, sy0, sy1, sz0, sz1, w_ref, z_ref, here_ref, sems):
    copies = []
    for q in range(EDGE // QUARTER):
        part = (slice(None), pl.ds(q * QUARTER, QUARTER))
        copies.append(pltpu.make_async_copy(c_ref.at[part], here_ref.at[part], sems.at[q]))
        copies[-1].start()
    for q, copy in enumerate(copies):
        copy.wait()
        for x in range(q * QUARTER, (q + 1) * QUARTER):
            got = [here_ref[f, x] for f in range(FIELDS)]
            for f, value in enumerate(primitives(*got)):
                w_ref[rows(f * EDGE + x), :] = value
    for f in range(FIELDS):
        depth = 4 if f == 4 else 2
        tiles = [w_ref[rows(f * EDGE + x), :] for x in range(EDGE)]
        z_ref[rows(f * EDGE, EDGE), :] = w_ref[rows(f * EDGE, EDGE), :].T
        turned_z = [z_tile(z_ref, f, z) for z in range(EDGE)]
        turned = (turned_z, swap_xy(tiles), tiles)
        for got, low, high in zip(turned, (sz0, sy0, sx0), (sz1, sy1, sx1)):
            for r in range(depth):
                low[rows(face_tile(f) + r), :] = got[r]
                high[rows(face_tile(f) + r), :] = got[EDGE - depth + r]


def device_position():
    place = lax.axis_index(AXES[0])
    for axis in AXES[1:]:
        place = place * lax.axis_size(axis) + lax.axis_index(axis)
    return place


def find_boxes(old_ref, new_ref):
    boxes = old_ref.shape[0]
    place = device_position()

    def halve(_, ends):
        low, high = ends
        middle = (low + high) // 2
        below = old_ref[jnp.minimum(middle, boxes - 1)] < place
        open_ends = low < high
        return (
            jnp.where(open_ends & below, middle + 1, low),
            jnp.where(open_ends & jnp.logical_not(below), middle, high),
        )

    ends = (jnp.int32(0), jnp.int32(boxes))
    for step in range(boxes.bit_length()):
        ends = halve(step, ends)
    low = ends[0]
    count = jnp.int32(0)
    for k in range(SLOTS):
        at = low + k
        mine = (at < boxes) & (old_ref[jnp.minimum(at, boxes - 1)] == place)
        count = count + mine.astype(jnp.int32)
    high = low + count
    before = jnp.maximum(low - 1, 0)
    after = jnp.minimum(high, boxes - 1)
    up_in = ((low > 0) & (new_ref[before] == place)).astype(jnp.int32)
    down_in = ((high < boxes) & (new_ref[after] == place)).astype(jnp.int32)
    down_out = (new_ref[low] == place - 1).astype(jnp.int32)
    up_out = (new_ref[high - 1] == place + 1).astype(jnp.int32)
    return low, count, up_in, down_in, down_out, up_out


def by_slot(values, axis=0):
    slot = iota(axis) & 3
    out = jnp.full((SUB, LANES), values[0])
    for b in range(1, SLOTS):
        out = jnp.where(slot == b, values[b], out)
    return out


def limited(p, fields):
    n = p.shape[0] - 6
    jump = jnp.abs(p[3 : n + 5] - p[1 : n + 3])
    flat = jnp.clip(1.0 - 2.0 * jump / (p[4 : n + 6] + p[0 : n + 2]), 0.0, 1.0)
    weight = 0.5 * jnp.minimum(jnp.minimum(flat[0:n], flat[1 : n + 1]), flat[2 : n + 2])
    left, right = [], []
    for w in fields:
        diff = w[1 : n + 2] - w[0 : n + 1]
        back, ahead = diff[0:n], diff[1 : n + 1]
        mean = 0.5 * (back + ahead)
        twice = diff + diff
        back2, ahead2 = twice[0:n], twice[1 : n + 1]
        rise = jnp.maximum(jnp.minimum(mean, jnp.minimum(back2, ahead2)), 0.0)
        fall = jnp.minimum(jnp.maximum(mean, jnp.maximum(back2, ahead2)), 0.0)
        shift = weight * (rise + fall)
        left.append(w[1 : n + 1] + shift)
        right.append(w[1 : n + 1] - shift)
    return left, right


def hllc(left, right):
    rho_l, u_l, v_l, w_l, p_l = left
    rho_r, u_r, v_r, w_r, p_r = right
    ratio_l = p_l / rho_l
    ratio_r = p_r / rho_r
    c_l = jnp.sqrt(1.4 * ratio_l)
    c_r = jnp.sqrt(1.4 * ratio_r)
    s_l = jnp.minimum(u_l - c_l, u_r - c_r)
    s_r = jnp.maximum(u_l + c_l, u_r + c_r)
    m_l = rho_l * (s_l - u_l)
    m_r = rho_r * (s_r - u_r)
    mid = (p_r - p_l + m_l * u_l - m_r * u_r) / (m_l - m_r)
    use_left = (s_l >= 0.0) | (mid >= 0.0)

    def pick(a, b):
        return jnp.where(use_left, a, b)

    rho, u, v, w, p = (
        pick(rho_l, rho_r),
        pick(u_l, u_r),
        pick(v_l, v_r),
        pick(w_l, w_r),
        pick(p_l, p_r),
    )
    ratio, mass = pick(ratio_l, ratio_r), pick(m_l, m_r)
    wave = pick(jnp.minimum(s_l, 0.0), jnp.maximum(s_r, 0.0))
    starred = wave != 0.0
    scale = jnp.where(starred, wave / jnp.where(starred, wave - mid, 1.0), 0.0)
    f_mass = rho * (u - wave) + scale * mass
    push = scale * (mid - u)
    energy = 2.5 * ratio + 0.5 * (u * u + v * v + w * w)
    return (
        f_mass,
        u * f_mass + push * mass + p,
        v * f_mass,
        w * f_mass,
        energy * f_mass + p * u + push * (mid * mass + p),
    )


def field_line(x_ref, y_ref, z_ref, axis, place, start, stop):
    field = ORDER[axis][place]
    if axis == 2:
        return jnp.stack([z_tile(z_ref, field, z) for z in range(start, stop)])
    return get(y_ref if axis else x_ref, field * EDGE + start, stop - start)


def inner_kernel(*refs):
    far = refs[0:5]
    w_ref, z_ref = refs[5:7]
    info_ref, index_ref, scale_ref, y_ref, flux_ref, edge_ref = refs[7:13]
    left_ref, right_ref = refs[13:15]
    old_ref, new_ref, level_ref, source_ref, coarse_ref = here = refs[15:20]
    sems = refs[20]
    copies = [pltpu.make_async_copy(a, b, sems.at[k]) for k, (a, b) in enumerate(zip(far, here))]
    for copy in copies:
        copy.start()

    for f in range(FIELDS):
        tiles = [w_ref[rows(f * EDGE + x), :] for x in range(EDGE)]
        for k, value in enumerate(swap_xy(tiles)):
            y_ref[rows(f * EDGE + k), :] = value
    for axis in range(3):
        lines = (w_ref, y_ref, z_ref, axis)
        p = field_line(*lines, 4, 0, EDGE)
        fields = [field_line(*lines, k, 2, INNER + 5) for k in range(FIELDS)]
        left, right = limited(p, fields)
        for k in range(FIELDS):
            put(left_ref, (k * 3 + axis) * INNER, left[k][0:INNER])
            put(right_ref, (k * 3 + axis) * INNER, right[k][1 : INNER + 1])
            put(edge_ref, (axis * 2) * FIELDS + k, right[k][0:1])
            put(edge_ref, (axis * 2 + 1) * FIELDS + k, left[k][INNER : INNER + 1])
    for copy in copies:
        copy.wait()
    low, count, up_in, down_in, down_out, up_out = find_boxes(old_ref, new_ref)
    boxes = old_ref.shape[0]
    staying = count - down_out - up_out
    info_ref[0] = count - 1
    slot = iota(0) & 3
    code = jnp.where(slot < up_in + staying, 1, jnp.where(slot < up_in + staying + down_in, 3, 0))
    index_ref[rows(18), :] = jnp.where(slot < up_in, 2, code)
    index_ref[rows(19), :] = (iota(0) & 4) + ((slot + down_out - up_in) & 3)
    steps = []
    for b in range(SLOTS):
        level = level_ref[jnp.minimum(low + b, boxes - 1)]
        steps.append(
            jnp.where(level == 0, 0.02, jnp.where(level == 1, 0.04, 0.08)).astype(jnp.float32)
        )
    scale_ref[...] = by_slot(steps)
    sub, lane = iota(0), iota(1)
    for face in range(6):
        along = 1 if face // 2 == 2 else 0
        source = by_slot([source_ref[b, face] for b in range(SLOTS)], along)
        codes = by_slot([coarse_ref[b, face] for b in range(SLOTS)], along)
        is_coarse = codes > 0
        quadrant = codes - 1
        first, second = (quadrant >> 1) & 1, quadrant & 1
        if along == 0:
            half = sub >> 2
            from_row = (source & 3) + 4 * jnp.where(is_coarse, first, half)
            near = (half * 4 + (lane >> 5)) * EDGE + second * 8 + ((lane & 15) >> 1)
            from_lane = jnp.where(is_coarse, near, lane)
        else:
            half = (lane >> 2) & 1
            from_row = jnp.where(is_coarse, half * 4 + (sub >> 1), sub)
            near = (first * 8 + (lane >> 4)) * 8 + second * 4
            from_lane = (source & 3) + jnp.where(is_coarse, near, lane & 124)
        index_ref[rows(3 * face), :] = from_row
        index_ref[rows(3 * face + 1), :] = from_lane
        index_ref[rows(3 * face + 2), :] = (source >> 2) + 2 * is_coarse.astype(jnp.int32)

    for step in range(3 * INNER // FACE_CHUNK):

        def load(ref):
            return [get(ref, k * 3 * INNER + step * FACE_CHUNK, FACE_CHUNK) for k in range(FIELDS)]

        for k, value in enumerate(hllc(load(left_ref), load(right_ref))):
            put(flux_ref, k * 3 * INNER + step * FACE_CHUNK, value)


def outer_kernel(*refs):
    far_ref, c_ref = refs[0:2]
    own, got = refs[2:8], refs[8:14]
    w_ref, z_ref, index_ref, scale_ref, y_ref, inner_ref, edge_ref = refs[14:21]
    new_ref, up_ref, down_ref = refs[21:24]
    ghost_ref, flux_ref, turn_ref, info_ref, sem = refs[24:29]
    copy = pltpu.make_async_copy(far_ref, info_ref, sem)
    copy.start()

    for face in range(6):
        axis, side = face // 2, face % 2
        from_row = index_ref[rows(3 * face), :]
        from_lane = index_ref[rows(3 * face + 1), :]
        flags = index_ref[rows(3 * face + 2), :]
        is_own = (flags & 1) == 1
        is_coarse = flags >= 2
        mine, theirs = own[2 * axis + 1 - side], got[face]
        turns = ((from_row, 0), (from_lane, 1))
        before, after = turns if axis < 2 else turns[::-1]
        for f in range(FIELDS):
            depth = 4 if f == 4 else 2
            picked = []
            for r in range(depth):
                place = rows(face_tile(f) + r)
                picked.append(
                    jnp.where(
                        is_own,
                        jnp.take_along_axis(mine[place, :], before[0], axis=before[1]),
                        jnp.take_along_axis(theirs[place, :], before[0], axis=before[1]),
                    )
                )
            for k in range(depth):
                source = picked[(depth // 2 if side == 0 else 0) + k // 2]
                chosen = jnp.where(is_coarse, source, picked[k])
                row = face * FACE_TILES + face_tile(ORDER[axis].index(f)) + k
                ghost_ref[rows(row), :] = jnp.take_along_axis(chosen, after[0], axis=after[1])

    for axis in range(3):
        for side in range(2):
            face = axis * 2 + side

            def line(k):
                depth = 4 if k == 4 else 2
                ghost = get(ghost_ref, face * FACE_TILES + face_tile(k), depth)
                near = (0, depth + 2) if side == 0 else (EDGE - depth - 2, EDGE)
                near = field_line(w_ref, y_ref, z_ref, axis, k, *near)
                return jnp.concatenate((ghost, near) if side == 0 else (near, ghost), axis=0)

            p = line(4)
            fields = [line(k) for k in range(4)] + [p[2:8]]
            left, right = limited(p, fields)
            edge = [get(edge_ref, face * FIELDS + k, 1) for k in range(FIELDS)]
            if side == 0:
                right = [jnp.concatenate([a[1:], b], axis=0) for a, b in zip(right, edge)]
            else:
                left = [jnp.concatenate([b, a[:-1]], axis=0) for a, b in zip(left, edge)]
            for k, value in enumerate(hllc(left, right)):
                put(flux_ref, (face * FIELDS + k) * OUTER, value)

    def change(axis, field):
        place = ORDER[axis].index(field)
        faces = [
            flux_ref[rows((axis * 2 * FIELDS + place) * OUTER + k), :] for k in range(OUTER)
        ]
        faces += [inner_ref[rows((place * 3 + axis) * INNER + k), :] for k in range(INNER)]
        faces += [
            flux_ref[rows(((axis * 2 + 1) * FIELDS + place) * OUTER + k), :] for k in range(OUTER)
        ]
        return [faces[k + 1] - faces[k] for k in range(EDGE)]

    scale = scale_ref[...]
    for f in range(FIELDS):
        along_x = change(0, f)
        along_y = swap_xy(change(1, f))
        along_z = from_z(change(2, f), turn_ref.at[rows(f * EDGE, EDGE)])
        for x in range(EDGE):
            total = along_x[x] + along_y[x] + along_z[x]
            place = rows(f * EDGE + x)
            new_ref[place, :] = c_ref[place, :] - scale * total
    copy.wait()
    for slot, out in ((info_ref[0], up_ref), (0, down_ref)):
        for t in range(2):
            for n in range(CELLS // SUB):
                out[rows(t * (CELLS // SUB) + n), :] = new_ref[
                    pl.ds(n * 64 + 4 * t + slot, SUB, stride=SUB), :
                ]


def settle_kernel(index_ref, new_ref, out_ref):
    stays = index_ref[rows(18), :] == 1
    from_row = index_ref[rows(19), :]
    for n in range(CELLS):
        value = jnp.take_along_axis(new_ref[rows(n), :], from_row, axis=0)
        out_ref[rows(n), :] = jnp.where(stays, value, 0.0)


def place_kernel(index_ref, settled_ref, lower_ref, upper_ref, out_ref, ready_ref, sems):
    code = index_ref[rows(18), :]
    first = iota(0) < 4
    from_lower, from_upper = code == 2, code == 3
    copies = []
    for f in range(FIELDS):
        for x in range(EDGE):
            n = f * EDGE + x

            def spread(ref):
                a = jnp.broadcast_to(ref[pl.ds(n, 1), :], (SUB, LANES))
                b = jnp.broadcast_to(ref[pl.ds(CELLS + n, 1), :], (SUB, LANES))
                return jnp.where(first, a, b)

            value = settled_ref[rows(n), :]
            value = jnp.where(from_lower, spread(lower_ref), value)
            value = jnp.where(from_upper, spread(upper_ref), value)
            for t in range(2):
                lanes = slice((2 * x + t) * LANES, (2 * x + t + 1) * LANES)
                ready_ref[f, :, lanes] = value[4 * t : 4 * t + 3]
        copies.append(pltpu.make_async_copy(ready_ref.at[f], out_ref.at[f], sems.at[f]))
        copies[-1].start()
    for copy in copies:
        copy.wait()


def shift_by(value, axis, step):
    count = 1
    for name in (axis,) if isinstance(axis, str) else axis:
        count *= lax.axis_size(name)
    return lax.ppermute(value, axis, [(i, (i + step) % count) for i in range(count)])


def tiles_of(count, dtype=jnp.float32):
    return jax.ShapeDtypeStruct((count * SUB, LANES), dtype)


def scratch(count):
    return pltpu.VMEM((count * SUB, LANES), jnp.float32)


def local(conserved, old_owner, new_owner, box_level, face_source, coarse_part):
    vmem = pl.BlockSpec(memory_space=pltpu.VMEM)
    smem = pl.BlockSpec(memory_space=pltpu.SMEM)
    hbm = pl.BlockSpec(memory_space=pltpu.HBM)
    params = pltpu.CompilerParams(vmem_limit_bytes=VMEM_LIMIT)
    cells = conserved.transpose(1, 0, 2).reshape(FIELDS, SLOTS, 2 * EDGE, LANES)
    cells = cells.transpose(0, 2, 1, 3)
    *sent, along_x, along_z = pl.pallas_call(
        layers_kernel,
        out_shape=[tiles_of(FACE_TILES)] * 6 + [tiles_of(CELLS)] * 2,
        in_specs=[hbm],
        out_specs=[vmem] * 8,
        scratch_shapes=[
            pltpu.VMEM((FIELDS, EDGE, SUB, LANES), jnp.float32),
            pltpu.SemaphoreType.DMA((EDGE // QUARTER,)),
        ],
        compiler_params=params,
        name="layers",
    )(cells.reshape(FIELDS, EDGE, SUB, LANES))
    got = [None] * 6
    for axis in range(3):
        got[2 * axis] = shift_by(sent[2 * axis + 1], AXES[axis], 1)
        got[2 * axis + 1] = shift_by(sent[2 * axis], AXES[axis], -1)
    small = (old_owner, new_owner, box_level, face_source, coarse_part)
    info, index, *inner = pl.pallas_call(
        inner_kernel,
        out_shape=[
            jax.ShapeDtypeStruct((8,), jnp.int32),
            tiles_of(20, jnp.int32),
            tiles_of(1),
            tiles_of(CELLS),
            tiles_of(FIELDS * 3 * INNER),
            tiles_of(6 * FIELDS),
        ],
        in_specs=[hbm] * 5 + [vmem] * 2,
        out_specs=[smem] + [vmem] * 5,
        scratch_shapes=[scratch(FIELDS * 3 * INNER)] * 2
        + [pltpu.SMEM(value.shape, jnp.int32) for value in small]
        + [pltpu.SemaphoreType.DMA((5,))],
        compiler_params=params,
        name="inner",
    )(*small, along_x, along_z)
    updated, upward, downward = pl.pallas_call(
        outer_kernel,
        out_shape=[tiles_of(CELLS), tiles_of(PACKED), tiles_of(PACKED)],
        in_specs=[pl.BlockSpec(memory_space=pl.ANY)] + [vmem] * 20,
        out_specs=[vmem] * 3,
        scratch_shapes=[
            scratch(6 * FACE_TILES),
            scratch(6 * FIELDS * OUTER),
            scratch(CELLS),
            pltpu.SMEM((8,), jnp.int32),
            pltpu.SemaphoreType.DMA(()),
        ],
        compiler_params=params,
        name="outer",
    )(info, cells.reshape(CELLS * SUB, LANES), *sent, *got, along_x, along_z, index, *inner)
    from_lower = shift_by(upward, AXES, 1)
    from_upper = shift_by(downward, AXES, -1)
    settled = pl.pallas_call(
        settle_kernel,
        out_shape=tiles_of(CELLS),
        in_specs=[vmem] * 2,
        out_specs=vmem,
        compiler_params=params,
        name="settle",
    )(index, updated)
    out_shape = (FIELDS, 3, EDGE**3)
    out = pl.pallas_call(
        place_kernel,
        out_shape=jax.ShapeDtypeStruct(out_shape, jnp.float32),
        in_specs=[vmem] * 4,
        out_specs=hbm,
        scratch_shapes=[
            pltpu.VMEM(out_shape, jnp.float32),
            pltpu.SemaphoreType.DMA((FIELDS,)),
        ],
        compiler_params=params,
        name="place",
    )(index, settled, from_lower, from_upper)
    return out.transpose(1, 0, 2)


def solution(mesh):
    return jax.shard_map(
        local,
        mesh=mesh,
        in_specs=(P(AXES, None, None), P(), P(), P(), P(AXES, None), P(AXES, None)),
        out_specs=P(AXES, None, None),
        check_vma=False,
    )
```

```python
import jax
import jax.numpy as jnp
from jax import lax
from jax.experimental import pallas as pl
from jax.experimental.pallas import tpu as pltpu
from jax.sharding import PartitionSpec as P

EDGE = 16
FIELDS = 5
LANES = 128
SUB = 8
SLOTS = 4
CELLS = FIELDS * EDGE
AXES = ("gx", "gy", "gz")
ORDER = ((0, 1, 2, 3, 4), (0, 2, 1, 3, 4), (0, 3, 1, 2, 4))
FACE_TILES = 12
INNER = 9
OUTER = 4
QUARTER = 4
FACE_CHUNK = 3
PACKED = 2 * CELLS // SUB
VMEM_LIMIT = 48 * 1024 * 1024


def iota(axis):
    return lax.broadcasted_iota(jnp.int32, (SUB, LANES), axis)


def rows(tile, count=1):
    start = tile * SUB
    if not isinstance(start, int):
        start = pl.multiple_of(start, SUB)
    return pl.ds(start, count * SUB)


def get(ref, tile, count):
    return ref[rows(tile, count), :].reshape(count, SUB, LANES)


def put(ref, tile, value):
    count = value.shape[0]
    ref[rows(tile, count), :] = value.reshape(count * SUB, LANES)


def swap_bit(tiles, bit, axis, step):
    low = (iota(axis) & step) == 0
    across = iota(axis) ^ step
    out = list(tiles)
    for i in range(len(tiles)):
        if i & bit:
            continue
        j = i | bit
        a, b = tiles[i], tiles[j]
        moving = jnp.where(low, b, a)
        if 2 * step == (SUB, LANES)[axis]:
            moved = pltpu.roll(moving, step, axis)
        else:
            moved = jnp.take_along_axis(moving, across, axis=axis)
        out[i] = jnp.where(low, a, moved)
        out[j] = jnp.where(low, moved, b)
    return out


def swap_xy(tiles):
    tiles = swap_bit(tiles, 8, 0, 4)
    for bit, step in ((4, 64), (2, 32), (1, 16)):
        tiles = swap_bit(tiles, bit, 1, step)
    return tiles


def z_tile(ref, field, z):
    return ref[pl.ds(field * EDGE * SUB + z, SUB, stride=EDGE), :]


def from_z(tiles, turn_ref):
    for z in range(EDGE):
        turn_ref[pl.ds(z, SUB, stride=EDGE), :] = tiles[z]
    whole = turn_ref[...].T
    return [whole[k * SUB : (k + 1) * SUB] for k in range(EDGE)]


def primitives(rho, mx, my, mz, energy):
    inv = 1.0 / rho
    u, v, w = mx * inv, my * inv, mz * inv
    p = 0.4 * (energy - 0.5 * rho * (u * u + v * v + w * w))
    return rho, u, v, w, p


def face_tile(field):
    return 2 * field


def is_even(axis):
    return lax.rem(lax.axis_index(axis), 2) == 0


def layers_kernel(c_ref, *refs):
    near, far = refs[0:3], refs[3:6]
    w_ref, z_ref, here_ref, sems = refs[6:10]
    even = [is_even(axis) for axis in AXES]
    copies = []
    for q in range(EDGE // QUARTER):
        part = (slice(None), pl.ds(q * QUARTER, QUARTER))
        copies.append(pltpu.make_async_copy(c_ref.at[part], here_ref.at[part], sems.at[q]))
        copies[-1].start()
    for q, copy in enumerate(copies):
        copy.wait()
        for x in range(q * QUARTER, (q + 1) * QUARTER):
            got = [here_ref[f, x] for f in range(FIELDS)]
            for f, value in enumerate(primitives(*got)):
                w_ref[rows(f * EDGE + x), :] = value
    for f in range(FIELDS):
        depth = 4 if f == 4 else 2
        tiles = [w_ref[rows(f * EDGE + x), :] for x in range(EDGE)]
        z_ref[rows(f * EDGE, EDGE), :] = w_ref[rows(f * EDGE, EDGE), :].T
        turned_z = [z_tile(z_ref, f, z) for z in range(EDGE)]
        turned = (tiles, swap_xy(tiles), turned_z)
        for axis in range(3):
            for r in range(depth):
                low, high = turned[axis][r], turned[axis][EDGE - depth + r]
                place = rows(face_tile(f) + r)
                near[axis][place, :] = jnp.where(even[axis], high, low)
                far[axis][place, :] = jnp.where(even[axis], low, high)


def device_position():
    place = lax.axis_index(AXES[0])
    for axis in AXES[1:]:
        place = place * lax.axis_size(axis) + lax.axis_index(axis)
    return place


def find_boxes(old_ref, new_ref):
    boxes = old_ref.shape[0]
    place = device_position()

    def halve(_, ends):
        low, high = ends
        middle = (low + high) // 2
        below = old_ref[jnp.minimum(middle, boxes - 1)] < place
        open_ends = low < high
        return (
            jnp.where(open_ends & below, middle + 1, low),
            jnp.where(open_ends & jnp.logical_not(below), middle, high),
        )

    ends = (jnp.int32(0), jnp.int32(boxes))
    for step in range(boxes.bit_length()):
        ends = halve(step, ends)
    low = ends[0]
    count = jnp.int32(0)
    for k in range(SLOTS):
        at = low + k
        mine = (at < boxes) & (old_ref[jnp.minimum(at, boxes - 1)] == place)
        count = count + mine.astype(jnp.int32)
    high = low + count
    before = jnp.maximum(low - 1, 0)
    after = jnp.minimum(high, boxes - 1)
    up_in = ((low > 0) & (new_ref[before] == place)).astype(jnp.int32)
    down_in = ((high < boxes) & (new_ref[after] == place)).astype(jnp.int32)
    down_out = (new_ref[low] == place - 1).astype(jnp.int32)
    up_out = (new_ref[high - 1] == place + 1).astype(jnp.int32)
    return low, count, up_in, down_in, down_out, up_out


def by_slot(values, axis=0):
    slot = iota(axis) & 3
    out = jnp.full((SUB, LANES), values[0])
    for b in range(1, SLOTS):
        out = jnp.where(slot == b, values[b], out)
    return out


def limited(p, fields):
    n = p.shape[0] - 6
    jump = jnp.abs(p[3 : n + 5] - p[1 : n + 3])
    flat = jnp.clip(1.0 - 2.0 * jump / (p[4 : n + 6] + p[0 : n + 2]), 0.0, 1.0)
    weight = 0.5 * jnp.minimum(jnp.minimum(flat[0:n], flat[1 : n + 1]), flat[2 : n + 2])
    left, right = [], []
    for w in fields:
        diff = w[1 : n + 2] - w[0 : n + 1]
        back, ahead = diff[0:n], diff[1 : n + 1]
        mean = 0.5 * (back + ahead)
        twice = diff + diff
        back2, ahead2 = twice[0:n], twice[1 : n + 1]
        rise = jnp.maximum(jnp.minimum(mean, jnp.minimum(back2, ahead2)), 0.0)
        fall = jnp.minimum(jnp.maximum(mean, jnp.maximum(back2, ahead2)), 0.0)
        shift = weight * (rise + fall)
        left.append(w[1 : n + 1] + shift)
        right.append(w[1 : n + 1] - shift)
    return left, right


def hllc(left, right):
    rho_l, u_l, v_l, w_l, p_l = left
    rho_r, u_r, v_r, w_r, p_r = right
    ratio_l = p_l / rho_l
    ratio_r = p_r / rho_r
    c_l = jnp.sqrt(1.4 * ratio_l)
    c_r = jnp.sqrt(1.4 * ratio_r)
    s_l = jnp.minimum(u_l - c_l, u_r - c_r)
    s_r = jnp.maximum(u_l + c_l, u_r + c_r)
    m_l = rho_l * (s_l - u_l)
    m_r = rho_r * (s_r - u_r)
    mid = (p_r - p_l + m_l * u_l - m_r * u_r) / (m_l - m_r)
    use_left = (s_l >= 0.0) | (mid >= 0.0)

    def pick(a, b):
        return jnp.where(use_left, a, b)

    rho, u, v, w, p = (
        pick(rho_l, rho_r),
        pick(u_l, u_r),
        pick(v_l, v_r),
        pick(w_l, w_r),
        pick(p_l, p_r),
    )
    ratio, mass = pick(ratio_l, ratio_r), pick(m_l, m_r)
    wave = pick(jnp.minimum(s_l, 0.0), jnp.maximum(s_r, 0.0))
    starred = wave != 0.0
    scale = jnp.where(starred, wave / jnp.where(starred, wave - mid, 1.0), 0.0)
    f_mass = rho * (u - wave) + scale * mass
    push = scale * (mid - u)
    energy = 2.5 * ratio + 0.5 * (u * u + v * v + w * w)
    return (
        f_mass,
        u * f_mass + push * mass + p,
        v * f_mass,
        w * f_mass,
        energy * f_mass + p * u + push * (mid * mass + p),
    )


def field_line(x_ref, y_ref, z_ref, axis, place, start, stop):
    field = ORDER[axis][place]
    if axis == 2:
        return jnp.stack([z_tile(z_ref, field, z) for z in range(start, stop)])
    return get(y_ref if axis else x_ref, field * EDGE + start, stop - start)


def inner_kernel(*refs):
    far = refs[0:5]
    w_ref, z_ref = refs[5:7]
    info_ref, index_ref, scale_ref, y_ref, flux_ref, edge_ref = refs[7:13]
    left_ref, right_ref = refs[13:15]
    old_ref, new_ref, level_ref, source_ref, coarse_ref = here = refs[15:20]
    sems = refs[20]
    copies = [pltpu.make_async_copy(a, b, sems.at[k]) for k, (a, b) in enumerate(zip(far, here))]
    for copy in copies:
        copy.start()

    for f in range(FIELDS):
        tiles = [w_ref[rows(f * EDGE + x), :] for x in range(EDGE)]
        for k, value in enumerate(swap_xy(tiles)):
            y_ref[rows(f * EDGE + k), :] = value
    for axis in range(3):
        lines = (w_ref, y_ref, z_ref, axis)
        p = field_line(*lines, 4, 0, EDGE)
        fields = [field_line(*lines, k, 2, INNER + 5) for k in range(FIELDS)]
        left, right = limited(p, fields)
        for k in range(FIELDS):
            put(left_ref, (k * 3 + axis) * INNER, left[k][0:INNER])
            put(right_ref, (k * 3 + axis) * INNER, right[k][1 : INNER + 1])
            put(edge_ref, (axis * 2) * FIELDS + k, right[k][0:1])
            put(edge_ref, (axis * 2 + 1) * FIELDS + k, left[k][INNER : INNER + 1])
    for copy in copies:
        copy.wait()
    low, count, up_in, down_in, down_out, up_out = find_boxes(old_ref, new_ref)
    boxes = old_ref.shape[0]
    staying = count - down_out - up_out
    info_ref[0] = count - 1
    slot = iota(0) & 3
    lower = jnp.where(is_even(AXES[-1]), 3, 2)
    taken = up_in + staying
    code = jnp.where(slot < taken, 1, jnp.where(slot < taken + down_in, 5 - lower, 0))
    index_ref[rows(18), :] = jnp.where(slot < up_in, lower, code)
    index_ref[rows(19), :] = (iota(0) & 4) + ((slot + down_out - up_in) & 3)
    steps = []
    for b in range(SLOTS):
        level = level_ref[jnp.minimum(low + b, boxes - 1)]
        steps.append(
            jnp.where(level == 0, 0.02, jnp.where(level == 1, 0.04, 0.08)).astype(jnp.float32)
        )
    scale_ref[...] = by_slot(steps)
    sub, lane = iota(0), iota(1)
    for face in range(6):
        along = 1 if face // 2 == 2 else 0
        source = by_slot([source_ref[b, face] for b in range(SLOTS)], along)
        codes = by_slot([coarse_ref[b, face] for b in range(SLOTS)], along)
        is_coarse = codes > 0
        quadrant = codes - 1
        first, second = (quadrant >> 1) & 1, quadrant & 1
        if along == 0:
            half = sub >> 2
            from_row = (source & 3) + 4 * jnp.where(is_coarse, first, half)
            near = (half * 4 + (lane >> 5)) * EDGE + second * 8 + ((lane & 15) >> 1)
            from_lane = jnp.where(is_coarse, near, lane)
        else:
            half = (lane >> 2) & 1
            from_row = jnp.where(is_coarse, half * 4 + (sub >> 1), sub)
            near = (first * 8 + (lane >> 4)) * 8 + second * 4
            from_lane = (source & 3) + jnp.where(is_coarse, near, lane & 124)
        index_ref[rows(3 * face), :] = from_row
        index_ref[rows(3 * face + 1), :] = from_lane
        index_ref[rows(3 * face + 2), :] = (source >> 2) + 2 * is_coarse.astype(jnp.int32)

    for step in range(3 * INNER // FACE_CHUNK):

        def load(ref):
            return [get(ref, k * 3 * INNER + step * FACE_CHUNK, FACE_CHUNK) for k in range(FIELDS)]

        for k, value in enumerate(hllc(load(left_ref), load(right_ref))):
            put(flux_ref, k * 3 * INNER + step * FACE_CHUNK, value)


def outer_kernel(*refs):
    sent_info_ref, c_ref = refs[0:2]
    near_got, far_got = refs[2:5], refs[5:8]
    w_ref, z_ref, index_ref, scale_ref, y_ref, inner_ref, edge_ref = refs[8:15]
    new_ref, near_ref, far_ref = refs[15:18]
    ghost_ref, flux_ref, turn_ref, info_ref, sem = refs[18:23]
    even = [is_even(axis) for axis in AXES]
    copy = pltpu.make_async_copy(sent_info_ref, info_ref, sem)
    copy.start()

    for face in range(6):
        axis, side = face // 2, face % 2
        from_row = index_ref[rows(3 * face), :]
        from_lane = index_ref[rows(3 * face + 1), :]
        flags = index_ref[rows(3 * face + 2), :]
        is_own = (flags & 1) == 1
        is_coarse = flags >= 2
        use_near = even[axis] if side == 1 else jnp.logical_not(even[axis])
        turns = ((from_row, 0), (from_lane, 1))
        before, after = turns if axis < 2 else turns[::-1]
        for f in range(FIELDS):
            depth = 4 if f == 4 else 2
            picked = []
            start = EDGE - depth if side == 0 else 0
            layer = (ORDER[axis].index(f), start, start + depth)
            own = field_line(w_ref, y_ref, z_ref, axis, *layer)
            for r in range(depth):
                place = rows(face_tile(f) + r)
                theirs = jnp.where(
                    use_near, near_got[axis][place, :], far_got[axis][place, :]
                )
                picked.append(
                    jnp.where(
                        is_own,
                        jnp.take_along_axis(own[r], before[0], axis=before[1]),
                        jnp.take_along_axis(theirs, before[0], axis=before[1]),
                    )
                )
            for k in range(depth):
                source = picked[(depth // 2 if side == 0 else 0) + k // 2]
                chosen = jnp.where(is_coarse, source, picked[k])
                row = face * FACE_TILES + face_tile(ORDER[axis].index(f)) + k
                ghost_ref[rows(row), :] = jnp.take_along_axis(chosen, after[0], axis=after[1])

    for axis in range(3):
        for side in range(2):
            face = axis * 2 + side

            def line(k):
                depth = 4 if k == 4 else 2
                ghost = get(ghost_ref, face * FACE_TILES + face_tile(k), depth)
                near = (0, depth + 2) if side == 0 else (EDGE - depth - 2, EDGE)
                near = field_line(w_ref, y_ref, z_ref, axis, k, *near)
                return jnp.concatenate((ghost, near) if side == 0 else (near, ghost), axis=0)

            p = line(4)
            fields = [line(k) for k in range(4)] + [p[2:8]]
            left, right = limited(p, fields)
            edge = [get(edge_ref, face * FIELDS + k, 1) for k in range(FIELDS)]
            if side == 0:
                right = [jnp.concatenate([a[1:], b], axis=0) for a, b in zip(right, edge)]
            else:
                left = [jnp.concatenate([b, a[:-1]], axis=0) for a, b in zip(left, edge)]
            for k, value in enumerate(hllc(left, right)):
                put(flux_ref, (face * FIELDS + k) * OUTER, value)

    def change(axis, field):
        place = ORDER[axis].index(field)
        faces = [
            flux_ref[rows((axis * 2 * FIELDS + place) * OUTER + k), :] for k in range(OUTER)
        ]
        faces += [inner_ref[rows((place * 3 + axis) * INNER + k), :] for k in range(INNER)]
        faces += [
            flux_ref[rows(((axis * 2 + 1) * FIELDS + place) * OUTER + k), :] for k in range(OUTER)
        ]
        return [faces[k + 1] - faces[k] for k in range(EDGE)]

    scale = scale_ref[...]
    for f in range(FIELDS):
        along_x = change(0, f)
        along_y = swap_xy(change(1, f))
        along_z = from_z(change(2, f), turn_ref.at[rows(f * EDGE, EDGE)])
        for x in range(EDGE):
            total = along_x[x] + along_y[x] + along_z[x]
            place = rows(f * EDGE + x)
            new_ref[place, :] = c_ref[place, :] - scale * total
    copy.wait()
    last = info_ref[0]
    up_near = even[2].astype(jnp.int32)
    for slot, out in ((last * up_near, near_ref), (last * (1 - up_near), far_ref)):
        for t in range(2):
            for n in range(CELLS // SUB):
                out[rows(t * (CELLS // SUB) + n), :] = new_ref[
                    pl.ds(n * 64 + 4 * t + slot, SUB, stride=SUB), :
                ]


def settle_kernel(index_ref, new_ref, out_ref):
    stays = index_ref[rows(18), :] == 1
    from_row = index_ref[rows(19), :]
    for n in range(CELLS):
        value = jnp.take_along_axis(new_ref[rows(n), :], from_row, axis=0)
        out_ref[rows(n), :] = jnp.where(stays, value, 0.0)


def place_kernel(index_ref, settled_ref, near_ref, far_ref, out_ref, ready_ref, sems):
    code = index_ref[rows(18), :]
    first = iota(0) < 4
    from_near, from_far = code == 2, code == 3
    copies = []
    for f in range(FIELDS):
        for x in range(EDGE):
            n = f * EDGE + x

            def spread(ref):
                a = jnp.broadcast_to(ref[pl.ds(n, 1), :], (SUB, LANES))
                b = jnp.broadcast_to(ref[pl.ds(CELLS + n, 1), :], (SUB, LANES))
                return jnp.where(first, a, b)

            value = settled_ref[rows(n), :]
            value = jnp.where(from_near, spread(near_ref), value)
            value = jnp.where(from_far, spread(far_ref), value)
            for t in range(2):
                lanes = slice((2 * x + t) * LANES, (2 * x + t + 1) * LANES)
                ready_ref[f, :, lanes] = value[4 * t : 4 * t + 3]
        copies.append(pltpu.make_async_copy(ready_ref.at[f], out_ref.at[f], sems.at[f]))
        copies[-1].start()
    for copy in copies:
        copy.wait()


def swap_with(value, axis, first):
    count = 1
    for name in (axis,) if isinstance(axis, str) else axis:
        count *= lax.axis_size(name)
    pairs = [(k, (k + 1) % count) for k in range(first, count, 2)]
    return lax.ppermute(value, axis, pairs + [(b, a) for a, b in pairs])


def tiles_of(count, dtype=jnp.float32):
    return jax.ShapeDtypeStruct((count * SUB, LANES), dtype)


def scratch(count):
    return pltpu.VMEM((count * SUB, LANES), jnp.float32)


def local(conserved, old_owner, new_owner, box_level, face_source, coarse_part):
    vmem = pl.BlockSpec(memory_space=pltpu.VMEM)
    smem = pl.BlockSpec(memory_space=pltpu.SMEM)
    hbm = pl.BlockSpec(memory_space=pltpu.HBM)
    params = pltpu.CompilerParams(vmem_limit_bytes=VMEM_LIMIT)
    cells = conserved.transpose(1, 0, 2).reshape(FIELDS, SLOTS, 2 * EDGE, LANES)
    cells = cells.transpose(0, 2, 1, 3)
    *sent, along_x, along_z = pl.pallas_call(
        layers_kernel,
        out_shape=[tiles_of(FACE_TILES)] * 6 + [tiles_of(CELLS)] * 2,
        in_specs=[hbm],
        out_specs=[vmem] * 8,
        scratch_shapes=[
            pltpu.VMEM((FIELDS, EDGE, SUB, LANES), jnp.float32),
            pltpu.SemaphoreType.DMA((EDGE // QUARTER,)),
        ],
        compiler_params=params,
        name="layers",
    )(cells.reshape(FIELDS, EDGE, SUB, LANES))
    far_got = [swap_with(value, axis, 1) for value, axis in zip(sent[3:6], AXES)]
    near_got = [swap_with(value, axis, 0) for value, axis in zip(sent[0:3], AXES)]
    small = (old_owner, new_owner, box_level, face_source, coarse_part)
    info, index, *inner = pl.pallas_call(
        inner_kernel,
        out_shape=[
            jax.ShapeDtypeStruct((8,), jnp.int32),
            tiles_of(20, jnp.int32),
            tiles_of(1),
            tiles_of(CELLS),
            tiles_of(FIELDS * 3 * INNER),
            tiles_of(6 * FIELDS),
        ],
        in_specs=[hbm] * 5 + [vmem] * 2,
        out_specs=[smem] + [vmem] * 5,
        scratch_shapes=[scratch(FIELDS * 3 * INNER)] * 2
        + [pltpu.SMEM(value.shape, jnp.int32) for value in small]
        + [pltpu.SemaphoreType.DMA((5,))],
        compiler_params=params,
        name="inner",
    )(*small, along_x, along_z)
    updated, near, far = pl.pallas_call(
        outer_kernel,
        out_shape=[tiles_of(CELLS), tiles_of(PACKED), tiles_of(PACKED)],
        in_specs=[pl.BlockSpec(memory_space=pl.ANY)] + [vmem] * 14,
        out_specs=[vmem] * 3,
        scratch_shapes=[
            scratch(6 * FACE_TILES),
            scratch(6 * FIELDS * OUTER),
            scratch(CELLS),
            pltpu.SMEM((8,), jnp.int32),
            pltpu.SemaphoreType.DMA(()),
        ],
        compiler_params=params,
        name="outer",
    )(
        info,
        cells.reshape(CELLS * SUB, LANES),
        *near_got,
        *far_got,
        along_x,
        along_z,
        index,
        *inner,
    )
    from_far = swap_with(far, AXES, 1)
    from_near = swap_with(near, AXES, 0)
    settled = pl.pallas_call(
        settle_kernel,
        out_shape=tiles_of(CELLS),
        in_specs=[vmem] * 2,
        out_specs=vmem,
        compiler_params=params,
        name="settle",
    )(index, updated)
    out_shape = (FIELDS, 3, EDGE**3)
    out = pl.pallas_call(
        place_kernel,
        out_shape=jax.ShapeDtypeStruct(out_shape, jnp.float32),
        in_specs=[vmem] * 4,
        out_specs=hbm,
        scratch_shapes=[
            pltpu.VMEM(out_shape, jnp.float32),
            pltpu.SemaphoreType.DMA((FIELDS,)),
        ],
        compiler_params=params,
        name="place",
    )(index, settled, from_near, from_far)
    return out.transpose(1, 0, 2)


def solution(mesh):
    return jax.shard_map(
        local,
        mesh=mesh,
        in_specs=(P(AXES, None, None), P(), P(), P(), P(AXES, None), P(AXES, None)),
        out_specs=P(AXES, None, None),
        check_vma=False,
    )
```

```python
import jax
import jax.numpy as jnp
from jax import lax
from jax.experimental import pallas as pl
from jax.experimental.pallas import tpu as pltpu
from jax.sharding import PartitionSpec as P

EDGE = 16
FIELDS = 5
LANES = 128
SUB = 8
SLOTS = 4
CELLS = FIELDS * EDGE
AXES = ("gx", "gy", "gz")
ORDER = ((0, 1, 2, 3, 4), (0, 2, 1, 3, 4), (0, 3, 1, 2, 4))
FACE_TILES = 12
INNER = 9
OUTER = 4
FACE_CHUNK = 3
PACKED = 2 * CELLS // SUB
VMEM_LIMIT = 48 * 1024 * 1024


def iota(axis):
    return lax.broadcasted_iota(jnp.int32, (SUB, LANES), axis)


def rows(tile, count=1):
    start = tile * SUB
    if not isinstance(start, int):
        start = pl.multiple_of(start, SUB)
    return pl.ds(start, count * SUB)


def get(ref, tile, count):
    return ref[rows(tile, count), :].reshape(count, SUB, LANES)


def put(ref, tile, value):
    count = value.shape[0]
    ref[rows(tile, count), :] = value.reshape(count * SUB, LANES)


def swap_bit(tiles, bit, axis, step):
    low = (iota(axis) & step) == 0
    across = iota(axis) ^ step
    out = list(tiles)
    for i in range(len(tiles)):
        if i & bit:
            continue
        j = i | bit
        a, b = tiles[i], tiles[j]
        moving = jnp.where(low, b, a)
        if 2 * step == (SUB, LANES)[axis]:
            moved = pltpu.roll(moving, step, axis)
        else:
            moved = jnp.take_along_axis(moving, across, axis=axis)
        out[i] = jnp.where(low, a, moved)
        out[j] = jnp.where(low, moved, b)
    return out


def swap_xy(tiles):
    tiles = swap_bit(tiles, 8, 0, 4)
    for bit, step in ((4, 64), (2, 32), (1, 16)):
        tiles = swap_bit(tiles, bit, 1, step)
    return tiles


def z_tile(ref, field, z):
    return ref[pl.ds(field * EDGE * SUB + z, SUB, stride=EDGE), :]


def from_z(tiles, turn_ref):
    for z in range(EDGE):
        turn_ref[pl.ds(z, SUB, stride=EDGE), :] = tiles[z]
    whole = turn_ref[...].T
    return [whole[k * SUB : (k + 1) * SUB] for k in range(EDGE)]


def primitives(rho, mx, my, mz, energy):
    inv = 1.0 / rho
    u, v, w = mx * inv, my * inv, mz * inv
    p = 0.4 * (energy - 0.5 * rho * (u * u + v * v + w * w))
    return rho, u, v, w, p


def face_tile(field):
    return 2 * field


def is_even(axis):
    return lax.rem(lax.axis_index(axis), 2) == 0


def layers_kernel(c_ref, *refs):
    near, far = refs[0:3], refs[3:6]
    w_ref, z_ref = refs[6:8]
    even = [is_even(axis) for axis in AXES]
    for x in range(EDGE):
        got = [c_ref[rows(f * EDGE + x), :] for f in range(FIELDS)]
        for f, value in enumerate(primitives(*got)):
            w_ref[rows(f * EDGE + x), :] = value
    for f in range(FIELDS):
        depth = 4 if f == 4 else 2
        tiles = [w_ref[rows(f * EDGE + x), :] for x in range(EDGE)]
        z_ref[rows(f * EDGE, EDGE), :] = w_ref[rows(f * EDGE, EDGE), :].T
        turned_z = [z_tile(z_ref, f, z) for z in range(EDGE)]
        turned = (tiles, swap_xy(tiles), turned_z)
        for axis in range(3):
            for r in range(depth):
                low, high = turned[axis][r], turned[axis][EDGE - depth + r]
                place = rows(face_tile(f) + r)
                near[axis][place, :] = jnp.where(even[axis], high, low)
                far[axis][place, :] = jnp.where(even[axis], low, high)


def device_position():
    place = lax.axis_index(AXES[0])
    for axis in AXES[1:]:
        place = place * lax.axis_size(axis) + lax.axis_index(axis)
    return place


def find_boxes(old_ref, new_ref):
    boxes = old_ref.shape[0]
    place = device_position()

    def halve(_, ends):
        low, high = ends
        middle = (low + high) // 2
        below = old_ref[jnp.minimum(middle, boxes - 1)] < place
        open_ends = low < high
        return (
            jnp.where(open_ends & below, middle + 1, low),
            jnp.where(open_ends & jnp.logical_not(below), middle, high),
        )

    ends = (jnp.int32(0), jnp.int32(boxes))
    for step in range(boxes.bit_length()):
        ends = halve(step, ends)
    low = ends[0]
    count = jnp.int32(0)
    for k in range(SLOTS):
        at = low + k
        mine = (at < boxes) & (old_ref[jnp.minimum(at, boxes - 1)] == place)
        count = count + mine.astype(jnp.int32)
    high = low + count
    before = jnp.maximum(low - 1, 0)
    after = jnp.minimum(high, boxes - 1)
    up_in = ((low > 0) & (new_ref[before] == place)).astype(jnp.int32)
    down_in = ((high < boxes) & (new_ref[after] == place)).astype(jnp.int32)
    down_out = (new_ref[low] == place - 1).astype(jnp.int32)
    up_out = (new_ref[high - 1] == place + 1).astype(jnp.int32)
    return low, count, up_in, down_in, down_out, up_out


def by_slot(values, axis=0):
    slot = iota(axis) & 3
    out = jnp.full((SUB, LANES), values[0])
    for b in range(1, SLOTS):
        out = jnp.where(slot == b, values[b], out)
    return out


def limited(p, fields):
    n = p.shape[0] - 6
    jump = jnp.abs(p[3 : n + 5] - p[1 : n + 3])
    flat = jnp.clip(1.0 - 2.0 * jump / (p[4 : n + 6] + p[0 : n + 2]), 0.0, 1.0)
    weight = 0.5 * jnp.minimum(jnp.minimum(flat[0:n], flat[1 : n + 1]), flat[2 : n + 2])
    left, right = [], []
    for w in fields:
        diff = w[1 : n + 2] - w[0 : n + 1]
        back, ahead = diff[0:n], diff[1 : n + 1]
        mean = 0.5 * (back + ahead)
        twice = diff + diff
        back2, ahead2 = twice[0:n], twice[1 : n + 1]
        rise = jnp.maximum(jnp.minimum(mean, jnp.minimum(back2, ahead2)), 0.0)
        fall = jnp.minimum(jnp.maximum(mean, jnp.maximum(back2, ahead2)), 0.0)
        shift = weight * (rise + fall)
        left.append(w[1 : n + 1] + shift)
        right.append(w[1 : n + 1] - shift)
    return left, right


def hllc(left, right):
    rho_l, u_l, v_l, w_l, p_l = left
    rho_r, u_r, v_r, w_r, p_r = right
    ratio_l = p_l / rho_l
    ratio_r = p_r / rho_r
    c_l = jnp.sqrt(1.4 * ratio_l)
    c_r = jnp.sqrt(1.4 * ratio_r)
    s_l = jnp.minimum(u_l - c_l, u_r - c_r)
    s_r = jnp.maximum(u_l + c_l, u_r + c_r)
    m_l = rho_l * (s_l - u_l)
    m_r = rho_r * (s_r - u_r)
    mid = (p_r - p_l + m_l * u_l - m_r * u_r) / (m_l - m_r)
    use_left = (s_l >= 0.0) | (mid >= 0.0)

    def pick(a, b):
        return jnp.where(use_left, a, b)

    rho, u, v, w, p = (
        pick(rho_l, rho_r),
        pick(u_l, u_r),
        pick(v_l, v_r),
        pick(w_l, w_r),
        pick(p_l, p_r),
    )
    ratio, mass = pick(ratio_l, ratio_r), pick(m_l, m_r)
    wave = pick(jnp.minimum(s_l, 0.0), jnp.maximum(s_r, 0.0))
    starred = wave != 0.0
    scale = jnp.where(starred, wave / jnp.where(starred, wave - mid, 1.0), 0.0)
    f_mass = rho * (u - wave) + scale * mass
    push = scale * (mid - u)
    energy = 2.5 * ratio + 0.5 * (u * u + v * v + w * w)
    return (
        f_mass,
        u * f_mass + push * mass + p,
        v * f_mass,
        w * f_mass,
        energy * f_mass + p * u + push * (mid * mass + p),
    )


def field_line(x_ref, y_ref, z_ref, axis, place, start, stop):
    field = ORDER[axis][place]
    if axis == 2:
        return jnp.stack([z_tile(z_ref, field, z) for z in range(start, stop)])
    return get(y_ref if axis else x_ref, field * EDGE + start, stop - start)


def inner_kernel(*refs):
    far = refs[0:5]
    w_ref, z_ref = refs[5:7]
    info_ref, index_ref, scale_ref, y_ref, flux_ref, edge_ref = refs[7:13]
    left_ref, right_ref = refs[13:15]
    old_ref, new_ref, level_ref, source_ref, coarse_ref = here = refs[15:20]
    sems = refs[20]
    copies = [pltpu.make_async_copy(a, b, sems.at[k]) for k, (a, b) in enumerate(zip(far, here))]
    for copy in copies:
        copy.start()

    for f in range(FIELDS):
        tiles = [w_ref[rows(f * EDGE + x), :] for x in range(EDGE)]
        for k, value in enumerate(swap_xy(tiles)):
            y_ref[rows(f * EDGE + k), :] = value
    for axis in range(3):
        lines = (w_ref, y_ref, z_ref, axis)
        p = field_line(*lines, 4, 0, EDGE)
        fields = [field_line(*lines, k, 2, INNER + 5) for k in range(FIELDS)]
        left, right = limited(p, fields)
        for k in range(FIELDS):
            put(left_ref, (k * 3 + axis) * INNER, left[k][0:INNER])
            put(right_ref, (k * 3 + axis) * INNER, right[k][1 : INNER + 1])
            put(edge_ref, (axis * 2) * FIELDS + k, right[k][0:1])
            put(edge_ref, (axis * 2 + 1) * FIELDS + k, left[k][INNER : INNER + 1])
    for copy in copies:
        copy.wait()
    low, count, up_in, down_in, down_out, up_out = find_boxes(old_ref, new_ref)
    boxes = old_ref.shape[0]
    staying = count - down_out - up_out
    info_ref[0] = count - 1
    slot = iota(0) & 3
    lower = jnp.where(is_even(AXES[-1]), 3, 2)
    taken = up_in + staying
    code = jnp.where(slot < taken, 1, jnp.where(slot < taken + down_in, 5 - lower, 0))
    index_ref[rows(18), :] = jnp.where(slot < up_in, lower, code)
    index_ref[rows(19), :] = (iota(0) & 4) + ((slot + down_out - up_in) & 3)
    steps = []
    for b in range(SLOTS):
        level = level_ref[jnp.minimum(low + b, boxes - 1)]
        steps.append(
            jnp.where(level == 0, 0.02, jnp.where(level == 1, 0.04, 0.08)).astype(jnp.float32)
        )
    scale_ref[...] = by_slot(steps)
    sub, lane = iota(0), iota(1)
    for face in range(6):
        along = 1 if face // 2 == 2 else 0
        source = by_slot([source_ref[b, face] for b in range(SLOTS)], along)
        codes = by_slot([coarse_ref[b, face] for b in range(SLOTS)], along)
        is_coarse = codes > 0
        quadrant = codes - 1
        first, second = (quadrant >> 1) & 1, quadrant & 1
        if along == 0:
            half = sub >> 2
            from_row = (source & 3) + 4 * jnp.where(is_coarse, first, half)
            near = (half * 4 + (lane >> 5)) * EDGE + second * 8 + ((lane & 15) >> 1)
            from_lane = jnp.where(is_coarse, near, lane)
        else:
            half = (lane >> 2) & 1
            from_row = jnp.where(is_coarse, half * 4 + (sub >> 1), sub)
            near = (first * 8 + (lane >> 4)) * 8 + second * 4
            from_lane = (source & 3) + jnp.where(is_coarse, near, lane & 124)
        index_ref[rows(3 * face), :] = from_row
        index_ref[rows(3 * face + 1), :] = from_lane
        index_ref[rows(3 * face + 2), :] = (source >> 2) + 2 * is_coarse.astype(jnp.int32)

    for step in range(3 * INNER // FACE_CHUNK):

        def load(ref):
            return [get(ref, k * 3 * INNER + step * FACE_CHUNK, FACE_CHUNK) for k in range(FIELDS)]

        for k, value in enumerate(hllc(load(left_ref), load(right_ref))):
            put(flux_ref, k * 3 * INNER + step * FACE_CHUNK, value)


def outer_kernel(*refs):
    sent_info_ref, c_ref = refs[0:2]
    near_got, far_got = refs[2:5], refs[5:8]
    w_ref, z_ref, index_ref, scale_ref, y_ref, inner_ref, edge_ref = refs[8:15]
    new_ref, near_ref, far_ref = refs[15:18]
    ghost_ref, flux_ref, turn_ref, info_ref, sem = refs[18:23]
    even = [is_even(axis) for axis in AXES]
    copy = pltpu.make_async_copy(sent_info_ref, info_ref, sem)
    copy.start()

    for face in range(6):
        axis, side = face // 2, face % 2
        from_row = index_ref[rows(3 * face), :]
        from_lane = index_ref[rows(3 * face + 1), :]
        flags = index_ref[rows(3 * face + 2), :]
        is_own = (flags & 1) == 1
        is_coarse = flags >= 2
        use_near = even[axis] if side == 1 else jnp.logical_not(even[axis])
        turns = ((from_row, 0), (from_lane, 1))
        before, after = turns if axis < 2 else turns[::-1]
        for f in range(FIELDS):
            depth = 4 if f == 4 else 2
            picked = []
            start = EDGE - depth if side == 0 else 0
            layer = (ORDER[axis].index(f), start, start + depth)
            own = field_line(w_ref, y_ref, z_ref, axis, *layer)
            for r in range(depth):
                place = rows(face_tile(f) + r)
                theirs = jnp.where(
                    use_near, near_got[axis][place, :], far_got[axis][place, :]
                )
                picked.append(
                    jnp.where(
                        is_own,
                        jnp.take_along_axis(own[r], before[0], axis=before[1]),
                        jnp.take_along_axis(theirs, before[0], axis=before[1]),
                    )
                )
            for k in range(depth):
                source = picked[(depth // 2 if side == 0 else 0) + k // 2]
                chosen = jnp.where(is_coarse, source, picked[k])
                row = face * FACE_TILES + face_tile(ORDER[axis].index(f)) + k
                ghost_ref[rows(row), :] = jnp.take_along_axis(chosen, after[0], axis=after[1])

    for axis in range(3):
        for side in range(2):
            face = axis * 2 + side

            def line(k):
                depth = 4 if k == 4 else 2
                ghost = get(ghost_ref, face * FACE_TILES + face_tile(k), depth)
                near = (0, depth + 2) if side == 0 else (EDGE - depth - 2, EDGE)
                near = field_line(w_ref, y_ref, z_ref, axis, k, *near)
                return jnp.concatenate((ghost, near) if side == 0 else (near, ghost), axis=0)

            p = line(4)
            fields = [line(k) for k in range(4)] + [p[2:8]]
            left, right = limited(p, fields)
            edge = [get(edge_ref, face * FIELDS + k, 1) for k in range(FIELDS)]
            if side == 0:
                right = [jnp.concatenate([a[1:], b], axis=0) for a, b in zip(right, edge)]
            else:
                left = [jnp.concatenate([b, a[:-1]], axis=0) for a, b in zip(left, edge)]
            for k, value in enumerate(hllc(left, right)):
                put(flux_ref, (face * FIELDS + k) * OUTER, value)

    def change(axis, field):
        place = ORDER[axis].index(field)
        faces = [
            flux_ref[rows((axis * 2 * FIELDS + place) * OUTER + k), :] for k in range(OUTER)
        ]
        faces += [inner_ref[rows((place * 3 + axis) * INNER + k), :] for k in range(INNER)]
        faces += [
            flux_ref[rows(((axis * 2 + 1) * FIELDS + place) * OUTER + k), :] for k in range(OUTER)
        ]
        return [faces[k + 1] - faces[k] for k in range(EDGE)]

    scale = scale_ref[...]
    for f in range(FIELDS):
        along_x = change(0, f)
        along_y = swap_xy(change(1, f))
        along_z = from_z(change(2, f), turn_ref.at[rows(f * EDGE, EDGE)])
        for x in range(EDGE):
            total = along_x[x] + along_y[x] + along_z[x]
            place = rows(f * EDGE + x)
            new_ref[place, :] = c_ref[place, :] - scale * total
    copy.wait()
    last = info_ref[0]
    up_near = even[2].astype(jnp.int32)
    for slot, out in ((last * up_near, near_ref), (last * (1 - up_near), far_ref)):
        for t in range(2):
            for n in range(CELLS // SUB):
                out[rows(t * (CELLS // SUB) + n), :] = new_ref[
                    pl.ds(n * 64 + 4 * t + slot, SUB, stride=SUB), :
                ]


def settle_kernel(index_ref, new_ref, out_ref):
    stays = index_ref[rows(18), :] == 1
    from_row = index_ref[rows(19), :]
    for n in range(CELLS):
        value = jnp.take_along_axis(new_ref[rows(n), :], from_row, axis=0)
        out_ref[rows(n), :] = jnp.where(stays, value, 0.0)


def place_kernel(index_ref, settled_ref, near_ref, far_ref, out_ref, ready_ref, sems):
    code = index_ref[rows(18), :]
    first = iota(0) < 4
    from_near, from_far = code == 2, code == 3
    copies = []
    for f in range(FIELDS):
        for x in range(EDGE):
            n = f * EDGE + x

            def spread(ref):
                a = jnp.broadcast_to(ref[pl.ds(n, 1), :], (SUB, LANES))
                b = jnp.broadcast_to(ref[pl.ds(CELLS + n, 1), :], (SUB, LANES))
                return jnp.where(first, a, b)

            value = settled_ref[rows(n), :]
            value = jnp.where(from_near, spread(near_ref), value)
            value = jnp.where(from_far, spread(far_ref), value)
            for t in range(2):
                lanes = slice((2 * x + t) * LANES, (2 * x + t + 1) * LANES)
                ready_ref[f, :, lanes] = value[4 * t : 4 * t + 3]
        copies.append(pltpu.make_async_copy(ready_ref.at[f], out_ref.at[f], sems.at[f]))
        copies[-1].start()
    for copy in copies:
        copy.wait()


def swap_with(value, axis, first):
    count = 1
    for name in (axis,) if isinstance(axis, str) else axis:
        count *= lax.axis_size(name)
    pairs = [(k, (k + 1) % count) for k in range(first, count, 2)]
    return lax.ppermute(value, axis, pairs + [(b, a) for a, b in pairs])


def tiles_of(count, dtype=jnp.float32):
    return jax.ShapeDtypeStruct((count * SUB, LANES), dtype)


def scratch(count):
    return pltpu.VMEM((count * SUB, LANES), jnp.float32)


def local(conserved, old_owner, new_owner, box_level, face_source, coarse_part):
    vmem = pl.BlockSpec(memory_space=pltpu.VMEM)
    smem = pl.BlockSpec(memory_space=pltpu.SMEM)
    hbm = pl.BlockSpec(memory_space=pltpu.HBM)
    params = pltpu.CompilerParams(vmem_limit_bytes=VMEM_LIMIT)
    cells = conserved.transpose(1, 0, 2).reshape(FIELDS, SLOTS, 2 * EDGE, LANES)
    cells = cells.transpose(0, 2, 1, 3).reshape(CELLS * SUB, LANES)
    *sent, along_x, along_z = pl.pallas_call(
        layers_kernel,
        out_shape=[tiles_of(FACE_TILES)] * 6 + [tiles_of(CELLS)] * 2,
        in_specs=[vmem],
        out_specs=[vmem] * 8,
        compiler_params=params,
        name="layers",
    )(cells)
    got = [swap_with(sent[k], AXES[k % 3], k // 3) for k in range(6)]
    small = (old_owner, new_owner, box_level, face_source, coarse_part)
    info, index, *inner = pl.pallas_call(
        inner_kernel,
        out_shape=[
            jax.ShapeDtypeStruct((8,), jnp.int32),
            tiles_of(20, jnp.int32),
            tiles_of(1),
            tiles_of(CELLS),
            tiles_of(FIELDS * 3 * INNER),
            tiles_of(6 * FIELDS),
        ],
        in_specs=[hbm] * 5 + [vmem] * 2,
        out_specs=[smem] + [vmem] * 5,
        scratch_shapes=[scratch(FIELDS * 3 * INNER)] * 2
        + [pltpu.SMEM(value.shape, jnp.int32) for value in small]
        + [pltpu.SemaphoreType.DMA((5,))],
        compiler_params=params,
        name="inner",
    )(*small, along_x, along_z)
    updated, near, far = pl.pallas_call(
        outer_kernel,
        out_shape=[tiles_of(CELLS), tiles_of(PACKED), tiles_of(PACKED)],
        in_specs=[pl.BlockSpec(memory_space=pl.ANY)] + [vmem] * 14,
        out_specs=[vmem] * 3,
        scratch_shapes=[
            scratch(6 * FACE_TILES),
            scratch(6 * FIELDS * OUTER),
            scratch(CELLS),
            pltpu.SMEM((8,), jnp.int32),
            pltpu.SemaphoreType.DMA(()),
        ],
        compiler_params=params,
        name="outer",
    )(
        info,
        cells,
        *got,
        along_x,
        along_z,
        index,
        *inner,
    )
    from_far = swap_with(far, AXES, 1)
    from_near = swap_with(near, AXES, 0)
    settled = pl.pallas_call(
        settle_kernel,
        out_shape=tiles_of(CELLS),
        in_specs=[vmem] * 2,
        out_specs=vmem,
        compiler_params=params,
        name="settle",
    )(index, updated)
    out_shape = (FIELDS, 3, EDGE**3)
    out = pl.pallas_call(
        place_kernel,
        out_shape=jax.ShapeDtypeStruct(out_shape, jnp.float32),
        in_specs=[vmem] * 4,
        out_specs=hbm,
        scratch_shapes=[
            pltpu.VMEM(out_shape, jnp.float32),
            pltpu.SemaphoreType.DMA((FIELDS,)),
        ],
        compiler_params=params,
        name="place",
    )(index, settled, from_near, from_far)
    return out.transpose(1, 0, 2)


def solution(mesh):
    return jax.shard_map(
        local,
        mesh=mesh,
        in_specs=(P(AXES, None, None), P(), P(), P(), P(AXES, None), P(AXES, None)),
        out_specs=P(AXES, None, None),
        check_vma=False,
    )
```

```python
import jax
import jax.numpy as jnp
from jax import lax
from jax.experimental import pallas as pl
from jax.experimental.pallas import tpu as pltpu
from jax.sharding import PartitionSpec as P

EDGE = 16
FIELDS = 5
LANES = 128
SUB = 8
SLOTS = 4
CELLS = FIELDS * EDGE
AXES = ("gx", "gy", "gz")
ORDER = ((0, 1, 2, 3, 4), (0, 2, 1, 3, 4), (0, 3, 1, 2, 4))
FACE_TILES = 12
INNER = 9
OUTER = 4
FACE_CHUNK = 9
PACKED = 2 * CELLS // SUB
VMEM_LIMIT = 48 * 1024 * 1024


def iota(axis):
    return lax.broadcasted_iota(jnp.int32, (SUB, LANES), axis)


def rows(tile, count=1):
    start = tile * SUB
    if not isinstance(start, int):
        start = pl.multiple_of(start, SUB)
    return pl.ds(start, count * SUB)


def get(ref, tile, count):
    return ref[rows(tile, count), :].reshape(count, SUB, LANES)


def put(ref, tile, value):
    count = value.shape[0]
    ref[rows(tile, count), :] = value.reshape(count * SUB, LANES)


def swap_bit(tiles, bit, axis, step):
    low = (iota(axis) & step) == 0
    across = iota(axis) ^ step
    out = list(tiles)
    for i in range(len(tiles)):
        if i & bit:
            continue
        j = i | bit
        a, b = tiles[i], tiles[j]
        moving = jnp.where(low, b, a)
        if 2 * step == (SUB, LANES)[axis]:
            moved = pltpu.roll(moving, step, axis)
        else:
            moved = jnp.take_along_axis(moving, across, axis=axis)
        out[i] = jnp.where(low, a, moved)
        out[j] = jnp.where(low, moved, b)
    return out


def swap_xy(tiles):
    tiles = swap_bit(tiles, 8, 0, 4)
    for bit, step in ((4, 64), (2, 32), (1, 16)):
        tiles = swap_bit(tiles, bit, 1, step)
    return tiles


def z_tile(ref, field, z):
    return ref[pl.ds(field * EDGE * SUB + z, SUB, stride=EDGE), :]


def from_z(tiles, turn_ref):
    for z in range(EDGE):
        turn_ref[pl.ds(z, SUB, stride=EDGE), :] = tiles[z]
    whole = turn_ref[...].T
    return [whole[k * SUB : (k + 1) * SUB] for k in range(EDGE)]


def primitives(rho, mx, my, mz, energy):
    inv = 1.0 / rho
    u, v, w = mx * inv, my * inv, mz * inv
    p = 0.4 * (energy - 0.5 * rho * (u * u + v * v + w * w))
    return rho, u, v, w, p


def face_tile(field):
    return 2 * field


def is_even(axis):
    return lax.rem(lax.axis_index(axis), 2) == 0


def layers_kernel(c_ref, *refs):
    near, far = refs[0:3], refs[3:6]
    w_ref, z_ref = refs[6:8]
    even = [is_even(axis) for axis in AXES]
    for x in range(EDGE):
        got = [c_ref[rows(f * EDGE + x), :] for f in range(FIELDS)]
        for f, value in enumerate(primitives(*got)):
            w_ref[rows(f * EDGE + x), :] = value
    for f in range(FIELDS):
        depth = 4 if f == 4 else 2
        tiles = [w_ref[rows(f * EDGE + x), :] for x in range(EDGE)]
        z_ref[rows(f * EDGE, EDGE), :] = w_ref[rows(f * EDGE, EDGE), :].T
        turned_z = [z_tile(z_ref, f, z) for z in range(EDGE)]
        turned = (tiles, swap_xy(tiles), turned_z)
        for axis in range(3):
            for r in range(depth):
                low, high = turned[axis][r], turned[axis][EDGE - depth + r]
                place = rows(face_tile(f) + r)
                near[axis][place, :] = jnp.where(even[axis], high, low)
                far[axis][place, :] = jnp.where(even[axis], low, high)


def device_position():
    place = lax.axis_index(AXES[0])
    for axis in AXES[1:]:
        place = place * lax.axis_size(axis) + lax.axis_index(axis)
    return place


def find_boxes(old_ref, new_ref):
    boxes = old_ref.shape[0]
    place = device_position()

    def halve(_, ends):
        low, high = ends
        middle = (low + high) // 2
        below = old_ref[jnp.minimum(middle, boxes - 1)] < place
        open_ends = low < high
        return (
            jnp.where(open_ends & below, middle + 1, low),
            jnp.where(open_ends & jnp.logical_not(below), middle, high),
        )

    ends = (jnp.int32(0), jnp.int32(boxes))
    for step in range(boxes.bit_length()):
        ends = halve(step, ends)
    low = ends[0]
    count = jnp.int32(0)
    for k in range(SLOTS):
        at = low + k
        mine = (at < boxes) & (old_ref[jnp.minimum(at, boxes - 1)] == place)
        count = count + mine.astype(jnp.int32)
    high = low + count
    before = jnp.maximum(low - 1, 0)
    after = jnp.minimum(high, boxes - 1)
    up_in = ((low > 0) & (new_ref[before] == place)).astype(jnp.int32)
    down_in = ((high < boxes) & (new_ref[after] == place)).astype(jnp.int32)
    down_out = (new_ref[low] == place - 1).astype(jnp.int32)
    up_out = (new_ref[high - 1] == place + 1).astype(jnp.int32)
    return low, count, up_in, down_in, down_out, up_out


def by_slot(values, axis=0):
    slot = iota(axis) & 3
    out = jnp.full((SUB, LANES), values[0])
    for b in range(1, SLOTS):
        out = jnp.where(slot == b, values[b], out)
    return out


def limited(p, fields):
    n = p.shape[0] - 6
    jump = jnp.abs(p[3 : n + 5] - p[1 : n + 3])
    flat = jnp.clip(1.0 - 2.0 * jump / (p[4 : n + 6] + p[0 : n + 2]), 0.0, 1.0)
    weight = 0.5 * jnp.minimum(jnp.minimum(flat[0:n], flat[1 : n + 1]), flat[2 : n + 2])
    left, right = [], []
    for w in fields:
        diff = w[1 : n + 2] - w[0 : n + 1]
        back, ahead = diff[0:n], diff[1 : n + 1]
        mean = 0.5 * (back + ahead)
        twice = diff + diff
        back2, ahead2 = twice[0:n], twice[1 : n + 1]
        rise = jnp.maximum(jnp.minimum(mean, jnp.minimum(back2, ahead2)), 0.0)
        fall = jnp.minimum(jnp.maximum(mean, jnp.maximum(back2, ahead2)), 0.0)
        shift = weight * (rise + fall)
        left.append(w[1 : n + 1] + shift)
        right.append(w[1 : n + 1] - shift)
    return left, right


def hllc(left, right):
    rho_l, u_l, v_l, w_l, p_l = left
    rho_r, u_r, v_r, w_r, p_r = right
    ratio_l = p_l / rho_l
    ratio_r = p_r / rho_r
    c_l = jnp.sqrt(1.4 * ratio_l)
    c_r = jnp.sqrt(1.4 * ratio_r)
    s_l = jnp.minimum(u_l - c_l, u_r - c_r)
    s_r = jnp.maximum(u_l + c_l, u_r + c_r)
    m_l = rho_l * (s_l - u_l)
    m_r = rho_r * (s_r - u_r)
    mid = (p_r - p_l + m_l * u_l - m_r * u_r) / (m_l - m_r)
    use_left = (s_l >= 0.0) | (mid >= 0.0)

    def pick(a, b):
        return jnp.where(use_left, a, b)

    rho, u, v, w, p = (
        pick(rho_l, rho_r),
        pick(u_l, u_r),
        pick(v_l, v_r),
        pick(w_l, w_r),
        pick(p_l, p_r),
    )
    ratio, mass = pick(ratio_l, ratio_r), pick(m_l, m_r)
    wave = pick(jnp.minimum(s_l, 0.0), jnp.maximum(s_r, 0.0))
    starred = wave != 0.0
    scale = jnp.where(starred, wave / jnp.where(starred, wave - mid, 1.0), 0.0)
    f_mass = rho * (u - wave) + scale * mass
    push = scale * (mid - u)
    energy = 2.5 * ratio + 0.5 * (u * u + v * v + w * w)
    return (
        f_mass,
        u * f_mass + push * mass + p,
        v * f_mass,
        w * f_mass,
        energy * f_mass + p * u + push * (mid * mass + p),
    )


def field_line(x_ref, y_ref, z_ref, axis, place, start, stop):
    field = ORDER[axis][place]
    if axis == 2:
        return jnp.stack([z_tile(z_ref, field, z) for z in range(start, stop)])
    return get(y_ref if axis else x_ref, field * EDGE + start, stop - start)


def inner_kernel(*refs):
    far = refs[0:5]
    w_ref, z_ref = refs[5:7]
    info_ref, index_ref, scale_ref, y_ref, flux_ref, edge_ref = refs[7:13]
    left_ref, right_ref = refs[13:15]
    old_ref, new_ref, level_ref, source_ref, coarse_ref = here = refs[15:20]
    sems = refs[20]
    copies = [pltpu.make_async_copy(a, b, sems.at[k]) for k, (a, b) in enumerate(zip(far, here))]
    for copy in copies:
        copy.start()

    for f in range(FIELDS):
        tiles = [w_ref[rows(f * EDGE + x), :] for x in range(EDGE)]
        for k, value in enumerate(swap_xy(tiles)):
            y_ref[rows(f * EDGE + k), :] = value
    for axis in range(3):
        lines = (w_ref, y_ref, z_ref, axis)
        p = field_line(*lines, 4, 0, EDGE)
        fields = [field_line(*lines, k, 2, INNER + 5) for k in range(FIELDS)]
        left, right = limited(p, fields)
        for k in range(FIELDS):
            put(left_ref, (k * 3 + axis) * INNER, left[k][0:INNER])
            put(right_ref, (k * 3 + axis) * INNER, right[k][1 : INNER + 1])
            put(edge_ref, (axis * 2) * FIELDS + k, right[k][0:1])
            put(edge_ref, (axis * 2 + 1) * FIELDS + k, left[k][INNER : INNER + 1])
    for copy in copies:
        copy.wait()
    low, count, up_in, down_in, down_out, up_out = find_boxes(old_ref, new_ref)
    boxes = old_ref.shape[0]
    staying = count - down_out - up_out
    info_ref[0] = count - 1
    slot = iota(0) & 3
    lower = jnp.where(is_even(AXES[-1]), 3, 2)
    taken = up_in + staying
    code = jnp.where(slot < taken, 1, jnp.where(slot < taken + down_in, 5 - lower, 0))
    index_ref[rows(18), :] = jnp.where(slot < up_in, lower, code)
    index_ref[rows(19), :] = (iota(0) & 4) + ((slot + down_out - up_in) & 3)
    steps = []
    for b in range(SLOTS):
        level = level_ref[jnp.minimum(low + b, boxes - 1)]
        steps.append(
            jnp.where(level == 0, 0.02, jnp.where(level == 1, 0.04, 0.08)).astype(jnp.float32)
        )
    scale_ref[...] = by_slot(steps)
    sub, lane = iota(0), iota(1)
    for face in range(6):
        along = 1 if face // 2 == 2 else 0
        source = by_slot([source_ref[b, face] for b in range(SLOTS)], along)
        codes = by_slot([coarse_ref[b, face] for b in range(SLOTS)], along)
        is_coarse = codes > 0
        quadrant = codes - 1
        first, second = (quadrant >> 1) & 1, quadrant & 1
        if along == 0:
            half = sub >> 2
            from_row = (source & 3) + 4 * jnp.where(is_coarse, first, half)
            near = (half * 4 + (lane >> 5)) * EDGE + second * 8 + ((lane & 15) >> 1)
            from_lane = jnp.where(is_coarse, near, lane)
        else:
            half = (lane >> 2) & 1
            from_row = jnp.where(is_coarse, half * 4 + (sub >> 1), sub)
            near = (first * 8 + (lane >> 4)) * 8 + second * 4
            from_lane = (source & 3) + jnp.where(is_coarse, near, lane & 124)
        index_ref[rows(3 * face), :] = from_row
        index_ref[rows(3 * face + 1), :] = from_lane
        index_ref[rows(3 * face + 2), :] = (source >> 2) + 2 * is_coarse.astype(jnp.int32)

    for step in range(3 * INNER // FACE_CHUNK):

        def load(ref):
            return [get(ref, k * 3 * INNER + step * FACE_CHUNK, FACE_CHUNK) for k in range(FIELDS)]

        for k, value in enumerate(hllc(load(left_ref), load(right_ref))):
            put(flux_ref, k * 3 * INNER + step * FACE_CHUNK, value)


def outer_kernel(*refs):
    sent_info_ref, c_ref = refs[0:2]
    near_got, far_got = refs[2:5], refs[5:8]
    w_ref, z_ref, index_ref, scale_ref, y_ref, inner_ref, edge_ref = refs[8:15]
    new_ref, near_ref, far_ref = refs[15:18]
    ghost_ref, flux_ref, turn_ref, info_ref, sem = refs[18:23]
    even = [is_even(axis) for axis in AXES]
    copy = pltpu.make_async_copy(sent_info_ref, info_ref, sem)
    copy.start()

    def fetch(face):
        axis, side = face // 2, face % 2
        from_row = index_ref[rows(3 * face), :]
        from_lane = index_ref[rows(3 * face + 1), :]
        flags = index_ref[rows(3 * face + 2), :]
        is_own = (flags & 1) == 1
        is_coarse = flags >= 2
        use_near = even[axis] if side == 1 else jnp.logical_not(even[axis])
        turns = ((from_row, 0), (from_lane, 1))
        before, after = turns if axis < 2 else turns[::-1]
        for f in range(FIELDS):
            depth = 4 if f == 4 else 2
            picked = []
            start = EDGE - depth if side == 0 else 0
            layer = (ORDER[axis].index(f), start, start + depth)
            own = field_line(w_ref, y_ref, z_ref, axis, *layer)
            for r in range(depth):
                place = rows(face_tile(f) + r)
                theirs = jnp.where(
                    use_near, near_got[axis][place, :], far_got[axis][place, :]
                )
                picked.append(
                    jnp.where(
                        is_own,
                        jnp.take_along_axis(own[r], before[0], axis=before[1]),
                        jnp.take_along_axis(theirs, before[0], axis=before[1]),
                    )
                )
            for k in range(depth):
                source = picked[(depth // 2 if side == 0 else 0) + k // 2]
                chosen = jnp.where(is_coarse, source, picked[k])
                row = face * FACE_TILES + face_tile(ORDER[axis].index(f)) + k
                ghost_ref[rows(row), :] = jnp.take_along_axis(chosen, after[0], axis=after[1])

    def edges(axis):
        for side in range(2):
            face = axis * 2 + side

            def line(k):
                depth = 4 if k == 4 else 2
                ghost = get(ghost_ref, face * FACE_TILES + face_tile(k), depth)
                near = (0, depth + 2) if side == 0 else (EDGE - depth - 2, EDGE)
                near = field_line(w_ref, y_ref, z_ref, axis, k, *near)
                return jnp.concatenate((ghost, near) if side == 0 else (near, ghost), axis=0)

            p = line(4)
            fields = [line(k) for k in range(4)] + [p[2:8]]
            left, right = limited(p, fields)
            edge = [get(edge_ref, face * FIELDS + k, 1) for k in range(FIELDS)]
            if side == 0:
                right = [jnp.concatenate([a[1:], b], axis=0) for a, b in zip(right, edge)]
            else:
                left = [jnp.concatenate([b, a[:-1]], axis=0) for a, b in zip(left, edge)]
            for k, value in enumerate(hllc(left, right)):
                put(flux_ref, (face * FIELDS + k) * OUTER, value)

    def change(axis, field):
        place = ORDER[axis].index(field)
        faces = [
            flux_ref[rows((axis * 2 * FIELDS + place) * OUTER + k), :] for k in range(OUTER)
        ]
        faces += [inner_ref[rows((place * 3 + axis) * INNER + k), :] for k in range(INNER)]
        faces += [
            flux_ref[rows(((axis * 2 + 1) * FIELDS + place) * OUTER + k), :] for k in range(OUTER)
        ]
        return [faces[k + 1] - faces[k] for k in range(EDGE)]

    fetch(4)
    fetch(5)
    fetch(2)
    fetch(3)
    edges(2)
    fetch(0)
    fetch(1)
    for f in range(FIELDS):
        tiles = from_z(change(2, f), turn_ref.at[rows(f * EDGE, EDGE)])
        turn_ref[rows(f * EDGE, EDGE), :] = jnp.concatenate(tiles, axis=0)
    edges(1)
    edges(0)
    scale = scale_ref[...]
    for f in range(FIELDS):
        along_x = change(0, f)
        along_y = swap_xy(change(1, f))
        for x in range(EDGE):
            place = rows(f * EDGE + x)
            total = along_x[x] + along_y[x] + turn_ref[place, :]
            new_ref[place, :] = c_ref[place, :] - scale * total
    copy.wait()
    last = info_ref[0]
    up_near = even[2].astype(jnp.int32)
    for slot, out in ((last * up_near, near_ref), (last * (1 - up_near), far_ref)):
        for t in range(2):
            for n in range(CELLS // SUB):
                out[rows(t * (CELLS // SUB) + n), :] = new_ref[
                    pl.ds(n * 64 + 4 * t + slot, SUB, stride=SUB), :
                ]


def settle_kernel(index_ref, new_ref, out_ref):
    stays = index_ref[rows(18), :] == 1
    from_row = index_ref[rows(19), :]
    for n in range(CELLS):
        value = jnp.take_along_axis(new_ref[rows(n), :], from_row, axis=0)
        out_ref[rows(n), :] = jnp.where(stays, value, 0.0)


def place_kernel(index_ref, settled_ref, near_ref, far_ref, out_ref, ready_ref, sems):
    code = index_ref[rows(18), :]
    first = iota(0) < 4
    from_near, from_far = code == 2, code == 3
    copies = []
    for f in range(FIELDS):
        for x in range(EDGE):
            n = f * EDGE + x

            def spread(ref):
                a = jnp.broadcast_to(ref[pl.ds(n, 1), :], (SUB, LANES))
                b = jnp.broadcast_to(ref[pl.ds(CELLS + n, 1), :], (SUB, LANES))
                return jnp.where(first, a, b)

            value = settled_ref[rows(n), :]
            value = jnp.where(from_near, spread(near_ref), value)
            value = jnp.where(from_far, spread(far_ref), value)
            for t in range(2):
                lanes = slice((2 * x + t) * LANES, (2 * x + t + 1) * LANES)
                ready_ref[f, :, lanes] = value[4 * t : 4 * t + 3]
        copies.append(pltpu.make_async_copy(ready_ref.at[f], out_ref.at[f], sems.at[f]))
        copies[-1].start()
    for copy in copies:
        copy.wait()


def swap_with(value, axis, first):
    count = 1
    for name in (axis,) if isinstance(axis, str) else axis:
        count *= lax.axis_size(name)
    pairs = [(k, (k + 1) % count) for k in range(first, count, 2)]
    return lax.ppermute(value, axis, pairs + [(b, a) for a, b in pairs])


def tiles_of(count, dtype=jnp.float32):
    return jax.ShapeDtypeStruct((count * SUB, LANES), dtype)


def scratch(count):
    return pltpu.VMEM((count * SUB, LANES), jnp.float32)


def local(conserved, old_owner, new_owner, box_level, face_source, coarse_part):
    vmem = pl.BlockSpec(memory_space=pltpu.VMEM)
    smem = pl.BlockSpec(memory_space=pltpu.SMEM)
    hbm = pl.BlockSpec(memory_space=pltpu.HBM)
    params = pltpu.CompilerParams(vmem_limit_bytes=VMEM_LIMIT)
    cells = conserved.transpose(1, 0, 2).reshape(FIELDS, SLOTS, 2 * EDGE, LANES)
    cells = cells.transpose(0, 2, 1, 3).reshape(CELLS * SUB, LANES)
    *sent, along_x, along_z = pl.pallas_call(
        layers_kernel,
        out_shape=[tiles_of(FACE_TILES)] * 6 + [tiles_of(CELLS)] * 2,
        in_specs=[vmem],
        out_specs=[vmem] * 8,
        compiler_params=params,
        name="layers",
    )(cells)
    got = [swap_with(sent[k], AXES[k % 3], k // 3) for k in range(6)]
    small = (old_owner, new_owner, box_level, face_source, coarse_part)
    info, index, *inner = pl.pallas_call(
        inner_kernel,
        out_shape=[
            jax.ShapeDtypeStruct((8,), jnp.int32),
            tiles_of(20, jnp.int32),
            tiles_of(1),
            tiles_of(CELLS),
            tiles_of(FIELDS * 3 * INNER),
            tiles_of(6 * FIELDS),
        ],
        in_specs=[hbm] * 5 + [vmem] * 2,
        out_specs=[smem] + [vmem] * 5,
        scratch_shapes=[scratch(FIELDS * 3 * INNER)] * 2
        + [pltpu.SMEM(value.shape, jnp.int32) for value in small]
        + [pltpu.SemaphoreType.DMA((5,))],
        compiler_params=params,
        name="inner",
    )(*small, along_x, along_z)
    updated, near, far = pl.pallas_call(
        outer_kernel,
        out_shape=[tiles_of(CELLS), tiles_of(PACKED), tiles_of(PACKED)],
        in_specs=[pl.BlockSpec(memory_space=pl.ANY)] + [vmem] * 14,
        out_specs=[vmem] * 3,
        scratch_shapes=[
            scratch(6 * FACE_TILES),
            scratch(6 * FIELDS * OUTER),
            scratch(CELLS),
            pltpu.SMEM((8,), jnp.int32),
            pltpu.SemaphoreType.DMA(()),
        ],
        compiler_params=params,
        name="outer",
    )(
        info,
        cells,
        *got,
        along_x,
        along_z,
        index,
        *inner,
    )
    from_far = swap_with(far, AXES, 1)
    from_near = swap_with(near, AXES, 0)
    settled = pl.pallas_call(
        settle_kernel,
        out_shape=tiles_of(CELLS),
        in_specs=[vmem] * 2,
        out_specs=vmem,
        compiler_params=params,
        name="settle",
    )(index, updated)
    out_shape = (FIELDS, 3, EDGE**3)
    out = pl.pallas_call(
        place_kernel,
        out_shape=jax.ShapeDtypeStruct(out_shape, jnp.float32),
        in_specs=[vmem] * 4,
        out_specs=hbm,
        scratch_shapes=[
            pltpu.VMEM(out_shape, jnp.float32),
            pltpu.SemaphoreType.DMA((FIELDS,)),
        ],
        compiler_params=params,
        name="place",
    )(index, settled, from_near, from_far)
    return out.transpose(1, 0, 2)


def solution(mesh):
    return jax.shard_map(
        local,
        mesh=mesh,
        in_specs=(P(AXES, None, None), P(), P(), P(), P(AXES, None), P(AXES, None)),
        out_specs=P(AXES, None, None),
        check_vma=False,
    )
```

```python
import jax
import jax.numpy as jnp
from jax import lax
from jax.experimental import pallas as pl
from jax.experimental.pallas import tpu as pltpu
from jax.sharding import PartitionSpec as P

EDGE = 16
FIELDS = 5
LANES = 128
SUB = 8
SLOTS = 4
CELLS = FIELDS * EDGE
AXES = ("gx", "gy", "gz")
ORDER = ((0, 1, 2, 3, 4), (0, 2, 1, 3, 4), (0, 3, 1, 2, 4))
FACE_TILES = 12
INNER = 9
OUTER = 4
FACE_CHUNK = 9
PACKED = 2 * CELLS // SUB
VMEM_LIMIT = 48 * 1024 * 1024


def iota(axis):
    return lax.broadcasted_iota(jnp.int32, (SUB, LANES), axis)


def rows(tile, count=1):
    start = tile * SUB
    if not isinstance(start, int):
        start = pl.multiple_of(start, SUB)
    return pl.ds(start, count * SUB)


def get(ref, tile, count):
    return ref[rows(tile, count), :].reshape(count, SUB, LANES)


def put(ref, tile, value):
    count = value.shape[0]
    ref[rows(tile, count), :] = value.reshape(count * SUB, LANES)


def swap_bit(tiles, bit, axis, step):
    low = (iota(axis) & step) == 0
    across = iota(axis) ^ step
    out = list(tiles)
    for i in range(len(tiles)):
        if i & bit:
            continue
        j = i | bit
        a, b = tiles[i], tiles[j]
        moving = jnp.where(low, b, a)
        if 2 * step == (SUB, LANES)[axis]:
            moved = pltpu.roll(moving, step, axis)
        else:
            moved = jnp.take_along_axis(moving, across, axis=axis)
        out[i] = jnp.where(low, a, moved)
        out[j] = jnp.where(low, moved, b)
    return out


def swap_xy(tiles):
    tiles = swap_bit(tiles, 8, 0, 4)
    for bit, step in ((4, 64), (2, 32), (1, 16)):
        tiles = swap_bit(tiles, bit, 1, step)
    return tiles


def z_tile(ref, field, z):
    return ref[pl.ds(field * EDGE * SUB + z, SUB, stride=EDGE), :]


def from_z(tiles, turn_ref):
    for z in range(EDGE):
        turn_ref[pl.ds(z, SUB, stride=EDGE), :] = tiles[z]
    whole = turn_ref[...].T
    return [whole[k * SUB : (k + 1) * SUB] for k in range(EDGE)]


def primitives(rho, mx, my, mz, energy):
    inv = 1.0 / rho
    u, v, w = mx * inv, my * inv, mz * inv
    p = 0.4 * (energy - 0.5 * rho * (u * u + v * v + w * w))
    return rho, u, v, w, p


def face_tile(field):
    return 2 * field


def is_even(axis):
    return lax.rem(lax.axis_index(axis), 2) == 0


def layers_kernel(c_ref, *refs):
    near, far = refs[0:3], refs[3:6]
    w_ref, z_ref = refs[6:8]
    even = [is_even(axis) for axis in AXES]
    for x in range(EDGE):
        got = [c_ref[rows(f * EDGE + x), :] for f in range(FIELDS)]
        for f, value in enumerate(primitives(*got)):
            w_ref[rows(f * EDGE + x), :] = value
    for f in range(FIELDS):
        depth = 4 if f == 4 else 2
        tiles = [w_ref[rows(f * EDGE + x), :] for x in range(EDGE)]
        z_ref[rows(f * EDGE, EDGE), :] = w_ref[rows(f * EDGE, EDGE), :].T
        turned_z = [z_tile(z_ref, f, z) for z in range(EDGE)]
        turned = (tiles, swap_xy(tiles), turned_z)
        for axis in range(3):
            for r in range(depth):
                low, high = turned[axis][r], turned[axis][EDGE - depth + r]
                place = rows(face_tile(f) + r)
                near[axis][place, :] = jnp.where(even[axis], high, low)
                far[axis][place, :] = jnp.where(even[axis], low, high)


def device_position():
    place = lax.axis_index(AXES[0])
    for axis in AXES[1:]:
        place = place * lax.axis_size(axis) + lax.axis_index(axis)
    return place


def find_boxes(old_ref, new_ref):
    boxes = old_ref.shape[0]
    place = device_position()

    def halve(_, ends):
        low, high = ends
        middle = (low + high) // 2
        below = old_ref[jnp.minimum(middle, boxes - 1)] < place
        open_ends = low < high
        return (
            jnp.where(open_ends & below, middle + 1, low),
            jnp.where(open_ends & jnp.logical_not(below), middle, high),
        )

    ends = (jnp.int32(0), jnp.int32(boxes))
    for step in range(boxes.bit_length()):
        ends = halve(step, ends)
    low = ends[0]
    count = jnp.int32(0)
    for k in range(SLOTS):
        at = low + k
        mine = (at < boxes) & (old_ref[jnp.minimum(at, boxes - 1)] == place)
        count = count + mine.astype(jnp.int32)
    high = low + count
    before = jnp.maximum(low - 1, 0)
    after = jnp.minimum(high, boxes - 1)
    up_in = ((low > 0) & (new_ref[before] == place)).astype(jnp.int32)
    down_in = ((high < boxes) & (new_ref[after] == place)).astype(jnp.int32)
    down_out = (new_ref[low] == place - 1).astype(jnp.int32)
    up_out = (new_ref[high - 1] == place + 1).astype(jnp.int32)
    return low, count, up_in, down_in, down_out, up_out


def by_slot(values, axis=0):
    slot = iota(axis) & 3
    out = jnp.full((SUB, LANES), values[0])
    for b in range(1, SLOTS):
        out = jnp.where(slot == b, values[b], out)
    return out


def limited(p, fields):
    n = p.shape[0] - 6
    jump = jnp.abs(p[3 : n + 5] - p[1 : n + 3])
    flat = jnp.clip(1.0 - 2.0 * jump / (p[4 : n + 6] + p[0 : n + 2]), 0.0, 1.0)
    weight = 0.5 * jnp.minimum(jnp.minimum(flat[0:n], flat[1 : n + 1]), flat[2 : n + 2])
    left, right = [], []
    for w in fields:
        diff = w[1 : n + 2] - w[0 : n + 1]
        back, ahead = diff[0:n], diff[1 : n + 1]
        mean = 0.5 * (back + ahead)
        twice = diff + diff
        back2, ahead2 = twice[0:n], twice[1 : n + 1]
        rise = jnp.maximum(jnp.minimum(mean, jnp.minimum(back2, ahead2)), 0.0)
        fall = jnp.minimum(jnp.maximum(mean, jnp.maximum(back2, ahead2)), 0.0)
        shift = weight * (rise + fall)
        left.append(w[1 : n + 1] + shift)
        right.append(w[1 : n + 1] - shift)
    return left, right


def hllc(left, right):
    rho_l, u_l, v_l, w_l, p_l = left
    rho_r, u_r, v_r, w_r, p_r = right
    ratio_l = p_l / rho_l
    ratio_r = p_r / rho_r
    c_l = jnp.sqrt(1.4 * ratio_l)
    c_r = jnp.sqrt(1.4 * ratio_r)
    s_l = jnp.minimum(u_l - c_l, u_r - c_r)
    s_r = jnp.maximum(u_l + c_l, u_r + c_r)
    m_l = rho_l * (s_l - u_l)
    m_r = rho_r * (s_r - u_r)
    mid = (p_r - p_l + m_l * u_l - m_r * u_r) / (m_l - m_r)
    use_left = (s_l >= 0.0) | (mid >= 0.0)

    def pick(a, b):
        return jnp.where(use_left, a, b)

    rho, u, v, w, p = (
        pick(rho_l, rho_r),
        pick(u_l, u_r),
        pick(v_l, v_r),
        pick(w_l, w_r),
        pick(p_l, p_r),
    )
    ratio, mass = pick(ratio_l, ratio_r), pick(m_l, m_r)
    wave = pick(jnp.minimum(s_l, 0.0), jnp.maximum(s_r, 0.0))
    starred = wave != 0.0
    scale = jnp.where(starred, wave / jnp.where(starred, wave - mid, 1.0), 0.0)
    f_mass = rho * (u - wave) + scale * mass
    push = scale * (mid - u)
    energy = 2.5 * ratio + 0.5 * (u * u + v * v + w * w)
    return (
        f_mass,
        u * f_mass + push * mass + p,
        v * f_mass,
        w * f_mass,
        energy * f_mass + p * u + push * (mid * mass + p),
    )


def field_line(x_ref, y_ref, z_ref, axis, place, start, stop):
    field = ORDER[axis][place]
    if axis == 2:
        return jnp.stack([z_tile(z_ref, field, z) for z in range(start, stop)])
    return get(y_ref if axis else x_ref, field * EDGE + start, stop - start)


def inner_kernel(*refs):
    far = refs[0:5]
    w_ref, z_ref = refs[5:7]
    info_ref, index_ref, scale_ref, y_ref, flux_ref, edge_ref = refs[7:13]
    left_ref, right_ref = refs[13:15]
    old_ref, new_ref, level_ref, source_ref, coarse_ref = here = refs[15:20]
    sems = refs[20]
    copies = [pltpu.make_async_copy(a, b, sems.at[k]) for k, (a, b) in enumerate(zip(far, here))]
    for copy in copies:
        copy.start()

    for f in range(FIELDS):
        tiles = [w_ref[rows(f * EDGE + x), :] for x in range(EDGE)]
        for k, value in enumerate(swap_xy(tiles)):
            y_ref[rows(f * EDGE + k), :] = value
    for axis in range(3):
        lines = (w_ref, y_ref, z_ref, axis)
        p = field_line(*lines, 4, 0, EDGE)
        fields = [field_line(*lines, k, 2, INNER + 5) for k in range(FIELDS)]
        left, right = limited(p, fields)
        for k in range(FIELDS):
            put(left_ref, (k * 3 + axis) * INNER, left[k][0:INNER])
            put(right_ref, (k * 3 + axis) * INNER, right[k][1 : INNER + 1])
            put(edge_ref, (axis * 2) * FIELDS + k, right[k][0:1])
            put(edge_ref, (axis * 2 + 1) * FIELDS + k, left[k][INNER : INNER + 1])
    for copy in copies:
        copy.wait()
    low, count, up_in, down_in, down_out, up_out = find_boxes(old_ref, new_ref)
    boxes = old_ref.shape[0]
    staying = count - down_out - up_out
    info_ref[0] = count - 1
    slot = iota(0) & 3
    lower = jnp.where(is_even(AXES[-1]), 3, 2)
    taken = up_in + staying
    code = jnp.where(slot < taken, 1, jnp.where(slot < taken + down_in, 5 - lower, 0))
    index_ref[rows(18), :] = jnp.where(slot < up_in, lower, code)
    index_ref[rows(19), :] = (iota(0) & 4) + ((slot + down_out - up_in) & 3)
    steps = []
    for b in range(SLOTS):
        level = level_ref[jnp.minimum(low + b, boxes - 1)]
        steps.append(
            jnp.where(level == 0, 0.02, jnp.where(level == 1, 0.04, 0.08)).astype(jnp.float32)
        )
    scale_ref[...] = by_slot(steps)
    sub, lane = iota(0), iota(1)
    for face in range(6):
        along = 1 if face // 2 == 2 else 0
        source = by_slot([source_ref[b, face] for b in range(SLOTS)], along)
        codes = by_slot([coarse_ref[b, face] for b in range(SLOTS)], along)
        is_coarse = codes > 0
        quadrant = codes - 1
        first, second = (quadrant >> 1) & 1, quadrant & 1
        if along == 0:
            half = sub >> 2
            from_row = (source & 3) + 4 * jnp.where(is_coarse, first, half)
            near = (half * 4 + (lane >> 5)) * EDGE + second * 8 + ((lane & 15) >> 1)
            from_lane = jnp.where(is_coarse, near, lane)
        else:
            half = (lane >> 2) & 1
            from_row = jnp.where(is_coarse, half * 4 + (sub >> 1), sub)
            near = (first * 8 + (lane >> 4)) * 8 + second * 4
            from_lane = (source & 3) + jnp.where(is_coarse, near, lane & 124)
        index_ref[rows(3 * face), :] = from_row
        index_ref[rows(3 * face + 1), :] = from_lane
        index_ref[rows(3 * face + 2), :] = (source >> 2) + 2 * is_coarse.astype(jnp.int32)

    for step in range(3 * INNER // FACE_CHUNK):

        def load(ref):
            return [get(ref, k * 3 * INNER + step * FACE_CHUNK, FACE_CHUNK) for k in range(FIELDS)]

        for k, value in enumerate(hllc(load(left_ref), load(right_ref))):
            put(flux_ref, k * 3 * INNER + step * FACE_CHUNK, value)


def outer_kernel(*refs):
    sent_info_ref, c_ref = refs[0:2]
    near_got, far_got = (refs[2], refs[4], refs[3]), refs[5:8]
    w_ref, z_ref, index_ref, scale_ref, y_ref, inner_ref, edge_ref = refs[8:15]
    new_ref, near_ref, far_ref = refs[15:18]
    ghost_ref, flux_ref, turn_ref, info_ref, sem = refs[18:23]
    even = [is_even(axis) for axis in AXES]
    copy = pltpu.make_async_copy(sent_info_ref, info_ref, sem)
    copy.start()

    def fetch(face):
        axis, side = face // 2, face % 2
        from_row = index_ref[rows(3 * face), :]
        from_lane = index_ref[rows(3 * face + 1), :]
        flags = index_ref[rows(3 * face + 2), :]
        is_own = (flags & 1) == 1
        is_coarse = flags >= 2
        use_near = even[axis] if side == 1 else jnp.logical_not(even[axis])
        turns = ((from_row, 0), (from_lane, 1))
        before, after = turns if axis < 2 else turns[::-1]
        for f in range(FIELDS):
            depth = 4 if f == 4 else 2
            picked = []
            start = EDGE - depth if side == 0 else 0
            layer = (ORDER[axis].index(f), start, start + depth)
            own = field_line(w_ref, y_ref, z_ref, axis, *layer)
            for r in range(depth):
                place = rows(face_tile(f) + r)
                theirs = jnp.where(
                    use_near, near_got[axis][place, :], far_got[axis][place, :]
                )
                picked.append(
                    jnp.where(
                        is_own,
                        jnp.take_along_axis(own[r], before[0], axis=before[1]),
                        jnp.take_along_axis(theirs, before[0], axis=before[1]),
                    )
                )
            for k in range(depth):
                source = picked[(depth // 2 if side == 0 else 0) + k // 2]
                chosen = jnp.where(is_coarse, source, picked[k])
                row = face * FACE_TILES + face_tile(ORDER[axis].index(f)) + k
                ghost_ref[rows(row), :] = jnp.take_along_axis(chosen, after[0], axis=after[1])

    def edges(axis):
        for side in range(2):
            face = axis * 2 + side

            def line(k):
                depth = 4 if k == 4 else 2
                ghost = get(ghost_ref, face * FACE_TILES + face_tile(k), depth)
                near = (0, depth + 2) if side == 0 else (EDGE - depth - 2, EDGE)
                near = field_line(w_ref, y_ref, z_ref, axis, k, *near)
                return jnp.concatenate((ghost, near) if side == 0 else (near, ghost), axis=0)

            p = line(4)
            fields = [line(k) for k in range(4)] + [p[2:8]]
            left, right = limited(p, fields)
            edge = [get(edge_ref, face * FIELDS + k, 1) for k in range(FIELDS)]
            if side == 0:
                right = [jnp.concatenate([a[1:], b], axis=0) for a, b in zip(right, edge)]
            else:
                left = [jnp.concatenate([b, a[:-1]], axis=0) for a, b in zip(left, edge)]
            for k, value in enumerate(hllc(left, right)):
                put(flux_ref, (face * FIELDS + k) * OUTER, value)

    def change(axis, field):
        place = ORDER[axis].index(field)
        faces = [
            flux_ref[rows((axis * 2 * FIELDS + place) * OUTER + k), :] for k in range(OUTER)
        ]
        faces += [inner_ref[rows((place * 3 + axis) * INNER + k), :] for k in range(INNER)]
        faces += [
            flux_ref[rows(((axis * 2 + 1) * FIELDS + place) * OUTER + k), :] for k in range(OUTER)
        ]
        return [faces[k + 1] - faces[k] for k in range(EDGE)]

    fetch(4)
    fetch(5)
    fetch(2)
    fetch(3)
    edges(2)
    fetch(0)
    fetch(1)
    for f in range(FIELDS):
        tiles = from_z(change(2, f), turn_ref.at[rows(f * EDGE, EDGE)])
        turn_ref[rows(f * EDGE, EDGE), :] = jnp.concatenate(tiles, axis=0)
    edges(1)
    edges(0)
    scale = scale_ref[...]
    for f in range(FIELDS):
        along_x = change(0, f)
        along_y = swap_xy(change(1, f))
        for x in range(EDGE):
            place = rows(f * EDGE + x)
            total = along_x[x] + along_y[x] + turn_ref[place, :]
            new_ref[place, :] = c_ref[place, :] - scale * total
    copy.wait()
    last = info_ref[0]
    up_near = even[2].astype(jnp.int32)
    for slot, out in ((last * up_near, near_ref), (last * (1 - up_near), far_ref)):
        for t in range(2):
            for n in range(CELLS // SUB):
                out[rows(t * (CELLS // SUB) + n), :] = new_ref[
                    pl.ds(n * 64 + 4 * t + slot, SUB, stride=SUB), :
                ]


def settle_kernel(index_ref, new_ref, out_ref):
    stays = index_ref[rows(18), :] == 1
    from_row = index_ref[rows(19), :]
    for n in range(CELLS):
        value = jnp.take_along_axis(new_ref[rows(n), :], from_row, axis=0)
        out_ref[rows(n), :] = jnp.where(stays, value, 0.0)


def place_kernel(index_ref, settled_ref, near_ref, far_ref, out_ref, ready_ref, sems):
    code = index_ref[rows(18), :]
    first = iota(0) < 4
    from_near, from_far = code == 2, code == 3
    copies = []
    for f in range(FIELDS):
        for x in range(EDGE):
            n = f * EDGE + x

            def spread(ref):
                a = jnp.broadcast_to(ref[pl.ds(n, 1), :], (SUB, LANES))
                b = jnp.broadcast_to(ref[pl.ds(CELLS + n, 1), :], (SUB, LANES))
                return jnp.where(first, a, b)

            value = settled_ref[rows(n), :]
            value = jnp.where(from_near, spread(near_ref), value)
            value = jnp.where(from_far, spread(far_ref), value)
            for t in range(2):
                lanes = slice((2 * x + t) * LANES, (2 * x + t + 1) * LANES)
                ready_ref[f, :, lanes] = value[4 * t : 4 * t + 3]
        copies.append(pltpu.make_async_copy(ready_ref.at[f], out_ref.at[f], sems.at[f]))
        copies[-1].start()
    for copy in copies:
        copy.wait()


def swap_with(value, axis, first):
    count = 1
    for name in (axis,) if isinstance(axis, str) else axis:
        count *= lax.axis_size(name)
    pairs = [(k, (k + 1) % count) for k in range(first, count, 2)]
    return lax.ppermute(value, axis, pairs + [(b, a) for a, b in pairs])


def tiles_of(count, dtype=jnp.float32):
    return jax.ShapeDtypeStruct((count * SUB, LANES), dtype)


def scratch(count):
    return pltpu.VMEM((count * SUB, LANES), jnp.float32)


def local(conserved, old_owner, new_owner, box_level, face_source, coarse_part):
    vmem = pl.BlockSpec(memory_space=pltpu.VMEM)
    smem = pl.BlockSpec(memory_space=pltpu.SMEM)
    hbm = pl.BlockSpec(memory_space=pltpu.HBM)
    params = pltpu.CompilerParams(vmem_limit_bytes=VMEM_LIMIT)
    cells = conserved.transpose(1, 0, 2).reshape(FIELDS, SLOTS, 2 * EDGE, LANES)
    cells = cells.transpose(0, 2, 1, 3).reshape(CELLS * SUB, LANES)
    *sent, along_x, along_z = pl.pallas_call(
        layers_kernel,
        out_shape=[tiles_of(FACE_TILES)] * 6 + [tiles_of(CELLS)] * 2,
        in_specs=[vmem],
        out_specs=[vmem] * 8,
        compiler_params=params,
        name="layers",
    )(cells)
    got = [swap_with(sent[k], AXES[k % 3], k // 3) for k in range(6)]
    small = (old_owner, new_owner, box_level, face_source, coarse_part)
    info, index, *inner = pl.pallas_call(
        inner_kernel,
        out_shape=[
            jax.ShapeDtypeStruct((8,), jnp.int32),
            tiles_of(20, jnp.int32),
            tiles_of(1),
            tiles_of(CELLS),
            tiles_of(FIELDS * 3 * INNER),
            tiles_of(6 * FIELDS),
        ],
        in_specs=[hbm] * 5 + [vmem] * 2,
        out_specs=[smem] + [vmem] * 5,
        scratch_shapes=[scratch(FIELDS * 3 * INNER)] * 2
        + [pltpu.SMEM(value.shape, jnp.int32) for value in small]
        + [pltpu.SemaphoreType.DMA((5,))],
        compiler_params=params,
        name="inner",
    )(*small, along_x, along_z)
    updated, near, far = pl.pallas_call(
        outer_kernel,
        out_shape=[tiles_of(CELLS), tiles_of(PACKED), tiles_of(PACKED)],
        in_specs=[pl.BlockSpec(memory_space=pl.ANY)] + [vmem] * 14,
        out_specs=[vmem] * 3,
        scratch_shapes=[
            scratch(6 * FACE_TILES),
            scratch(6 * FIELDS * OUTER),
            scratch(CELLS),
            pltpu.SMEM((8,), jnp.int32),
            pltpu.SemaphoreType.DMA(()),
        ],
        compiler_params=params,
        name="outer",
    )(
        info,
        cells,
        *(got[k] for k in (0, 2, 1, 3, 4, 5)),
        along_x,
        along_z,
        index,
        *inner,
    )
    from_far = swap_with(far, AXES, 1)
    from_near = swap_with(near, AXES, 0)
    settled = pl.pallas_call(
        settle_kernel,
        out_shape=tiles_of(CELLS),
        in_specs=[vmem] * 2,
        out_specs=vmem,
        compiler_params=params,
        name="settle",
    )(index, updated)
    out_shape = (FIELDS, 3, EDGE**3)
    out = pl.pallas_call(
        place_kernel,
        out_shape=jax.ShapeDtypeStruct(out_shape, jnp.float32),
        in_specs=[vmem] * 4,
        out_specs=hbm,
        scratch_shapes=[
            pltpu.VMEM(out_shape, jnp.float32),
            pltpu.SemaphoreType.DMA((FIELDS,)),
        ],
        compiler_params=params,
        name="place",
    )(index, settled, from_near, from_far)
    return out.transpose(1, 0, 2)


def solution(mesh):
    return jax.shard_map(
        local,
        mesh=mesh,
        in_specs=(P(AXES, None, None), P(), P(), P(), P(AXES, None), P(AXES, None)),
        out_specs=P(AXES, None, None),
        check_vma=False,
    )
```
